128 devices in a mesh: code: 4 (over y), row: 32 (over z, x, core).
Axes of the slice: x: 4, y: 4, z: 4, core: 2. Of those that a mesh axis runs over, the one named last changes fastest.
Arguments:
- residuals: bfloat16 [131072, 768], P(('code', 'row')), may hold values from -40 to 40
- codes: int32 [131072], P(('code', 'row')), may hold values from 0 to 7, as said below
- counts: int32 [4, 32, 4], P('code', 'row'), may hold values from 0 to 512, as said below
- centroids: float32 [8, 256, 768], P('code'), may hold values from -4 to 4
Outputs:
- centroids_out: float32 [8, 256, 768], P('code')
- residual_out: float32 [4, 32, 2048, 768], P('code', 'row')
The draws below stay inside these ranges and needn't reach their ends.
Inputs may be any that keep to these rules, and one draw needn't show every extreme that they name: `counts`: each shard sends exactly 512 rows to one owner group and splits the rest among the others; all shards with index j = 0 along `row` send their 512 rows to the same owner group. `codes`: the rows of a shard are ordered by owner group code // 2, group 0 first, in blocks of the sizes given by counts.
All inputs are finite; a program needn't handle non-finite values.
Results may differ from the reference program's by a relative error of at most 0.0024.
Values may be sent and summed in bfloat16 or wider, within the bound.
A program may use at most 64 MiB of HBM per device.

```python
import jax
import jax.numpy as jnp
from jax import lax

D = 768
SUBCODES = 256
GROUP_CODES = 2
ROWS_DEV = 1024
ITERS = 3
CAP = 512
CODES = 8
ROWS = 131072
N_CODE = 4
N_ROW = 32


def route_tables(key):
    hot_key, cut_key, code_key = jax.random.split(key, 3)
    half = ROWS_DEV // 2
    hot = jax.random.randint(hot_key, (N_CODE, N_ROW), 0, N_CODE)
    shared = jax.random.randint(jax.random.fold_in(hot_key, 7), (), 0, N_CODE)
    hot = hot.at[:, 0].set(shared)
    cuts = jnp.sort(jax.random.randint(cut_key, (N_CODE, N_ROW, N_CODE - 2), 0, half + 1), axis=-1)
    edges = jnp.concatenate([jnp.zeros((N_CODE, N_ROW, 1), jnp.int32), cuts, jnp.full((N_CODE, N_ROW, 1), half, jnp.int32)], -1)
    pieces = edges[..., 1:] - edges[..., :-1]
    owner = jnp.arange(N_CODE, dtype=jnp.int32)
    place = owner[None, None, :] - (owner[None, None, :] > hot[..., None]).astype(jnp.int32)
    place = jnp.clip(place, 0, N_CODE - 2)
    other = jnp.take_along_axis(pieces, place, -1)
    counts = jnp.where(owner[None, None, :] == hot[..., None], half, other).astype(jnp.int32)
    ends = jnp.cumsum(counts, -1)
    position = jnp.arange(ROWS_DEV, dtype=jnp.int32)
    group = jnp.sum((position[None, None, :, None] >= ends[:, :, None, :]).astype(jnp.int32), -1)
    within = jax.random.randint(code_key, (N_CODE, N_ROW, ROWS_DEV), 0, GROUP_CODES)
    codes = (group * GROUP_CODES + within).reshape(-1).astype(jnp.int32)
    return (counts, codes)


def normal_table(key):
    key = jax.random.fold_in(key, 6)
    return jnp.clip(0.5 * jax.random.normal(key, (CODES, SUBCODES, D), jnp.float32), -4.0, 4.0)


def band_pull(key, codes, table):
    shard_row = jnp.arange(ROWS, dtype=jnp.int32) // ROWS_DEV % N_ROW
    offset = jax.random.randint(jax.random.fold_in(key, 11), (ROWS,), 0, max(SUBCODES // 8, 1))
    chosen = (shard_row * SUBCODES // N_ROW + offset) % SUBCODES
    return table[codes, chosen]


def draw_counts(key, part):
    return route_tables(key)[0]


def draw_codes(key, part):
    return route_tables(key)[1]


def draw_centroids(key, part):
    return normal_table(jax.random.fold_in(key, 13))


def draw_residuals(key, part):
    counts, codes = route_tables(key)
    table = normal_table(key)
    pull = band_pull(key, codes, table)
    key = jax.random.fold_in(key, 8)
    keys = jax.random.split(key, 3)
    rowscale = jnp.exp(jax.random.uniform(keys[0], (ROWS, 1), jnp.float32, jnp.log(0.4), jnp.log(4.0)))
    colscale = jnp.exp(jax.random.uniform(keys[1], (1, D), jnp.float32, jnp.log(0.4), jnp.log(2.5)))
    base = jnp.clip(jax.random.normal(keys[2], (ROWS, D), jnp.float32), -4.0, 4.0)
    return jnp.clip(base * rowscale * colscale + 1.2 * pull, -40.0, 40.0).astype(jnp.bfloat16)


def setup_inputs(seed: int = 0) -> dict:
    seeds = jax.random.split(jax.random.key(seed), 5)
    return {
        "residuals": draw_residuals(jax.random.fold_in(seeds[4], 71), 0),
        "codes": draw_codes(jax.random.fold_in(seeds[4], 71), 0),
        "counts": draw_counts(jax.random.fold_in(seeds[4], 71), 0),
        "centroids": draw_centroids(jax.random.fold_in(seeds[4], 71), 0),
    }


score_scale = 0.0625


def owner_rows(residuals, codes, counts, group):
    shards = N_CODE * N_ROW
    width = residuals.shape[1]
    rows = residuals.reshape(shards, ROWS_DEV, width)
    rows = jnp.concatenate([rows, jnp.zeros((shards, CAP, width), rows.dtype)], 1)
    labels = codes.reshape(shards, ROWS_DEV)
    labels = jnp.concatenate([labels, jnp.zeros((shards, CAP), jnp.int32)], 1)
    sends = counts.reshape(shards, N_CODE)
    starts = (jnp.cumsum(sends, 1) - sends).astype(jnp.int32)
    begin = jnp.take(starts, group, axis=1).astype(jnp.int32)
    amount = jnp.take(sends, group, axis=1)
    slot = jnp.arange(CAP, dtype=jnp.int32)

    def one(block, names, first, number):
        piece = lax.dynamic_slice_in_dim(block, first, CAP, 0)
        tags = lax.dynamic_slice_in_dim(names, first, CAP, 0)
        live = slot < number
        return jnp.where(live[:, None], piece, jnp.zeros_like(piece)), jnp.where(live, tags - group * GROUP_CODES, -1)

    piece, tags = jax.vmap(one)(rows, labels, begin, amount)
    piece = piece.reshape(N_CODE, N_ROW, CAP, width).transpose(1, 0, 2, 3).reshape(N_ROW * N_CODE * CAP, width)
    tags = tags.reshape(N_CODE, N_ROW, CAP).transpose(1, 0, 2).reshape(N_ROW * N_CODE * CAP)
    return piece, tags


def group_level(rows, tags, cent):
    member = (tags[:, None] == jnp.arange(GROUP_CODES, dtype=jnp.int32)[None, :]).astype(jnp.float32)
    valid = jnp.sum(member, 1)
    width = rows.shape[1]
    rows_wide = rows.astype(jnp.float32)
    weight = None
    for step in range(ITERS):
        flat = cent.reshape(GROUP_CODES * SUBCODES, width)
        cnorm = jnp.sum(flat * flat, 1).reshape(GROUP_CODES, SUBCODES)
        raw = jnp.dot(rows_wide, flat.T, precision=lax.Precision.HIGHEST, preferred_element_type=jnp.float32).reshape(-1, GROUP_CODES, SUBCODES)
        scores = jnp.sum(member[:, :, None] * (score_scale * (2.0 * raw - cnorm[None])), 1)
        top = jnp.max(scores, 1, keepdims=True)
        expo = jnp.exp(scores - top)
        first = expo / jnp.sum(expo, 1, keepdims=True) * valid[:, None]
        col = jnp.sum(member[:, :, None] * first[:, None, :], 0)
        colrow = jnp.sum(member[:, :, None] * col[None], 1) + (1.0 - valid)[:, None]
        quot = first / colrow
        prob = quot / (jnp.sum(quot, 1, keepdims=True) + (1.0 - valid)[:, None])
        weight = (member[:, :, None] * prob[:, None, :]).reshape(-1, GROUP_CODES * SUBCODES)
        num = jnp.dot(weight.T, rows_wide, precision=lax.Precision.HIGHEST, preferred_element_type=jnp.float32)
        mass = jnp.sum(weight, 0)
        cent = (num / mass[:, None]).reshape(GROUP_CODES, SUBCODES, width)
    final = cent.reshape(GROUP_CODES * SUBCODES, width)
    recon = jnp.dot(weight, final, precision=lax.Precision.HIGHEST, preferred_element_type=jnp.float32)
    resid = rows_wide - recon
    return cent, resid


def reference(residuals, codes, counts, centroids):
    width = residuals.shape[1]
    start = centroids.reshape(N_CODE, GROUP_CODES, SUBCODES, width)

    def per_group(inputs):
        group, cent = inputs
        rows, tags = owner_rows(residuals, codes, counts, group)
        return group_level(rows, tags, cent)

    cents, resid = lax.map(per_group, (jnp.arange(N_CODE, dtype=jnp.int32), start))
    return cents.reshape(CODES, SUBCODES, width), resid.reshape(N_CODE, N_ROW, N_CODE * CAP, width)
```

```python
import jax
import jax.numpy as jnp
from jax import lax
from jax.experimental import pallas as pl
from jax.experimental.pallas import tpu as pltpu
from jax.sharding import PartitionSpec as P

ITERS = 3
SCORE_SCALE = 0.0625
LOG2E = 1.4426950408889634
MESH = pl.DeviceIdType.MESH
GROUPS = 4
CHIPS = 16
SIDE = 4
LANES = 128
CAP = 512
CHUNK = 128
F32 = jnp.float32
BF16 = jnp.bfloat16

NT = (((1,), (1,)), ((), ()))
TN = (((0,), (0,)), ((), ()))


def wait_bytes(ref, sem):
    pltpu.make_async_copy(ref, ref, sem).wait()


def kernel(
    x_hbm, codes_ref, counts_ref, cent_hbm, cout_ref, rout_ref,
    x_ref, cent_ref, sendbuf, sendtag, rows, tags, p0, phi, plo, colsend, colrecv, numsend, numrecv,
    massacc, massrecv, call, chi, clo, cn, colacc, pother, cother, res,
    in_sem, asend, tsend, arecv, trecv, fsend, ftsend, frecv, ftrecv,
    col_s, col_r, rs_s, rs_r, m_s, m_r, ag_s, ag_r, po_s, po_r, co_s, co_r, out_sem,
):
    i = lax.axis_index("code")
    j = lax.axis_index("row")
    core = lax.rem(j, 2)
    chip = lax.div(j, 2)
    cz = lax.div(chip, SIDE)
    cx = lax.rem(chip, SIDE)
    sib = (i, 2 * chip + 1 - core)
    share = numrecv.shape[1]
    clusters = call.shape[0]
    width = call.shape[1]

    def chip_at(d):
        return lax.rem(cz + lax.div(d, SIDE), SIDE) * SIDE + lax.rem(cx + lax.rem(d, SIDE), SIDE)

    def row_peer(t):
        return (i, 2 * t + core)

    def group(d):
        return lax.rem(i + d, GROUPS)

    load_x = pltpu.make_async_copy(x_hbm, x_ref, in_sem.at[0])
    load_x.start()
    load_c = pltpu.make_async_copy(cent_hbm.at[core], cent_ref, in_sem.at[1])
    load_c.start()

    barrier = pltpu.get_barrier_semaphore()
    for d in range(1, GROUPS):
        pl.semaphore_signal(barrier, inc=1, device_id=(group(d), j), device_id_type=MESH)
    pl.semaphore_signal(barrier, inc=1, device_id=sib, device_id_type=MESH)

    def greet(d, carry):
        pl.semaphore_signal(barrier, inc=1, device_id=row_peer(chip_at(d)), device_id_type=MESH)
        return carry

    lax.fori_loop(1, CHIPS, greet, 0)

    load_x.wait()
    half = CAP // 2
    iota_r = lax.broadcasted_iota(jnp.int32, (half, x_ref.shape[0]), 1)
    iota_t = lax.broadcasted_iota(jnp.int32, (half, x_ref.shape[0]), 0)
    diff = iota_r - iota_t
    codes8 = jnp.broadcast_to(codes_ref[...], (8, codes_ref.shape[1]))

    def block(d, h):
        target = group(d)
        start = jnp.int32(0)
        for g in range(GROUPS - 1):
            start = start + jnp.where(g < target, counts_ref[g], 0)
        number = counts_ref[target] - h * half
        pick = jnp.where((diff == start + h * half) & (iota_t < number), 1.0, 0.0).astype(BF16)
        piece = jnp.dot(pick, x_ref[...], preferred_element_type=F32).astype(BF16)
        label = (codes8 - 2 * target + 1).astype(F32).astype(BF16)
        tag = lax.dot_general(label, pick, NT, preferred_element_type=F32)
        return piece, tag

    def a2a_copy(d, q):
        lines = pl.ds(q * CHUNK, CHUNK)
        return pltpu.make_async_remote_copy(
            sendbuf.at[d - 1, lines], rows.at[core * GROUPS + d, lines], asend, arecv.at[d - 1, q],
            device_id=(group(d), j), device_id_type=MESH,
        )

    def tag_copy(d):
        return pltpu.make_async_remote_copy(
            sendtag.at[d - 1], tags.at[core * GROUPS + d], tsend, trecv.at[d - 1],
            device_id=(group(d), j), device_id_type=MESH,
        )

    def forward_copy(d, q):
        lines = pl.ds(q * CHUNK, CHUNK)
        return pltpu.make_async_remote_copy(
            rows.at[core * GROUPS + d, lines], rows.at[core * GROUPS + d, lines], fsend, frecv.at[d, q],
            device_id=sib, device_id_type=MESH,
        )

    def forward_tag(d):
        return pltpu.make_async_remote_copy(
            tags.at[core * GROUPS + d], tags.at[core * GROUPS + d], ftsend, ftrecv.at[d],
            device_id=sib, device_id_type=MESH,
        )

    quarters = CAP // CHUNK
    first = True
    for h in range(2):
        for d in (2, 1, 3):
            piece, tag = block(d, h)
            sendbuf[d - 1, h * half : (h + 1) * half, :] = piece
            sendtag[d - 1, :, h * half : (h + 1) * half] = tag
            if first:
                pl.semaphore_wait(barrier, GROUPS - 1 + 1 + CHIPS - 1)
                first = False
            if h == 1:
                tag_copy(d).start()
            for q in range(quarters // 2):
                a2a_copy(d, h * (quarters // 2) + q).start()
    for h in range(2):
        piece, tag = block(0, h)
        rows[core * GROUPS, h * half : (h + 1) * half, :] = piece
        tags[core * GROUPS, :, h * half : (h + 1) * half] = tag
    forward_tag(0).start()

    def own_forward(q, carry):
        forward_copy(0, q).start()
        return carry

    lax.fori_loop(0, quarters, own_forward, 0)

    def split(c):
        hi = c.astype(BF16)
        chi[...] = hi
        clo[...] = (c - hi.astype(F32)).astype(BF16)
        norm = jnp.sum(c * c, axis=1, keepdims=True) * (SCORE_SCALE * LOG2E)
        cn[...] = jnp.broadcast_to(norm, cn.shape)

    def first_soft(b, lo, n):
        x = rows[b, pl.ds(lo, n), :]
        s = lax.dot_general(chi[...], x, NT, preferred_element_type=F32)
        s = s + lax.dot_general(clo[...], x, NT, preferred_element_type=F32)
        for k in range(n // LANES):
            at = pl.ds(lo + k * LANES, LANES)
            t = s[:, k * LANES : (k + 1) * LANES] * (2.0 * SCORE_SCALE * LOG2E) - cn[...]
            e = jnp.exp2(t - jnp.max(t, axis=0, keepdims=True))
            total = jnp.sum(e, axis=0, keepdims=True)
            live = tags[b, 0:1, at] == (core + 1).astype(F32)
            p = e * jnp.where(live, 1.0 / total, 0.0)
            p0[b, :, at] = p
            colacc[...] += p

    load_c.wait()
    split(cent_ref[...])
    colacc[...] = jnp.zeros_like(colacc)

    other = 1 - core

    def own_soft(q, carry):
        lo = pl.multiple_of(q * CHUNK, CHUNK)
        first_soft(core * GROUPS, lo, CHUNK)
        return carry

    lax.fori_loop(0, quarters, own_soft, 0)
    forward_tag(0).wait_recv()

    def sib_soft(q, carry):
        lo = pl.multiple_of(q * CHUNK, CHUNK)
        forward_copy(0, q).wait_recv()
        first_soft(other * GROUPS, lo, CHUNK)
        return carry

    lax.fori_loop(0, quarters, sib_soft, 0)

    for d in (2, 1, 3):
        tag_copy(d).wait_recv()
        forward_tag(d).start()

    def sib_tag(d, carry):
        forward_tag(d).wait_recv()
        return carry

    lax.fori_loop(1, GROUPS, sib_tag, 0)

    def arrive(t, carry):
        q = lax.div(t, GROUPS - 1)
        d = lax.rem(t, GROUPS - 1) + 1
        lo = pl.multiple_of(q * CHUNK, CHUNK)
        a2a_copy(d, q).wait_recv()
        forward_copy(d, q).start()
        first_soft(core * GROUPS + d, lo, CHUNK)
        forward_copy(d, q).wait_recv()
        first_soft(other * GROUPS + d, lo, CHUNK)
        return carry

    lax.fori_loop(0, quarters * (GROUPS - 1), arrive, 0)

    def chunk_of(t):
        return pl.ds(pl.multiple_of(t * share, share), share)

    mine = chunk_of(chip)

    def col_copy(d):
        return pltpu.make_async_remote_copy(
            colsend, colrecv.at[d - 1], col_s, col_r, device_id=row_peer(chip_at(d)), device_id_type=MESH
        )

    def rs_copy(d):
        t = chip_at(d)
        return pltpu.make_async_remote_copy(
            numsend.at[chunk_of(t)], numrecv.at[d - 1], rs_s, rs_r, device_id=row_peer(t), device_id_type=MESH
        )

    def mass_copy(d):
        t = chip_at(d)
        return pltpu.make_async_remote_copy(
            massacc.at[chunk_of(t)], massrecv.at[d - 1], m_s, m_r, device_id=row_peer(t), device_id_type=MESH
        )

    def ag_copy(d):
        return pltpu.make_async_remote_copy(
            call.at[mine], call.at[mine], ag_s, ag_r, device_id=row_peer(chip_at(d)), device_id_type=MESH
        )

    def each_peer(make):
        def body(d, carry):
            make(d).start()
            return carry

        lax.fori_loop(1, CHIPS, body, 0)

    blocks = 2 * GROUPS
    rest = pl.ds(0, (CHIPS - 1) * share)

    def update(step, carry):
        acc = jnp.transpose(colacc[...])
        colsend[...] = jnp.sum(acc.reshape(LANES // 8, 8, clusters), axis=0)
        each_peer(col_copy)
        massacc[...] = jnp.zeros_like(massacc)
        wait_bytes(colrecv, col_r)
        col = colsend[...] + jnp.sum(colrecv[...], axis=0)
        inverse = 1.0 / jnp.sum(col, axis=0, keepdims=True)
        icol = jnp.transpose(jnp.broadcast_to(inverse, (LANES, clusters)))
        colacc[...] = icol

        def weigh(b, carry):
            for k in range(CAP // LANES):
                at = slice(k * LANES, (k + 1) * LANES)
                q = p0[b, :, at] * colacc[...]
                total = jnp.sum(q, axis=0, keepdims=True)
                live = tags[b, 0:1, at] == (core + 1).astype(F32)
                p = q * jnp.where(live, 1.0 / jnp.where(live, total, 1.0), 0.0)
                hi = p.astype(BF16)
                phi[b, :, at] = hi
                plo[b, :, at] = (p - hi.astype(F32)).astype(BF16)
                massacc[...] += p
            x = rows[b]
            part = jnp.dot(phi[b], x, preferred_element_type=F32)
            part = part + jnp.dot(plo[b], x, preferred_element_type=F32)

            @pl.when(b == 0)
            def _():
                numsend[...] = part

            @pl.when(b > 0)
            def _():
                numsend[...] += part

            return carry

        lax.fori_loop(0, blocks, weigh, 0)
        each_peer(rs_copy)
        each_peer(mass_copy)
        wait_bytes(colrecv, col_s)
        wait_bytes(massrecv, m_r)
        wait_bytes(numrecv, rs_r)
        mass = massacc[mine, :] + jnp.sum(massrecv[...], axis=0)
        num = numsend[mine, :] + jnp.sum(numrecv[...], axis=0)
        call[mine, :] = num / jnp.sum(mass, axis=1, keepdims=True)
        each_peer(ag_copy)
        wait_bytes(massrecv, m_s)
        wait_bytes(numrecv, rs_s)
        wait_bytes(call.at[rest], ag_r)
        wait_bytes(call.at[rest], ag_s)
        split(call[...])

        @pl.when(step < ITERS - 1)
        def _():
            colacc[...] = jnp.zeros_like(colacc)

            def soft(b, carry):
                first_soft(b, 0, CAP)
                return carry

            lax.fori_loop(0, blocks, soft, 0)

        return carry

    lax.fori_loop(0, ITERS, update, 0)

    pcopy = pltpu.make_async_remote_copy(
        phi.at[pl.ds(other * GROUPS, GROUPS)], pother, po_s, po_r, device_id=sib, device_id_type=MESH
    )
    pcopy.start()
    ccopy = pltpu.make_async_remote_copy(call, cother, co_s, co_r, device_id=sib, device_id_type=MESH)
    ccopy.start()
    own_out = pltpu.make_async_copy(call, cout_ref.at[core], in_sem.at[0])
    own_out.start()
    wait_bytes(sendbuf, asend)
    wait_bytes(sendtag, tsend)
    wait_bytes(rows.at[pl.ds(0, GROUPS)], fsend)
    wait_bytes(tags.at[pl.ds(0, GROUPS)], ftsend)
    pcopy.wait()
    ccopy.wait()
    other_out = pltpu.make_async_copy(cother, cout_ref.at[other], in_sem.at[1])
    other_out.start()
    ohi = cother[...].astype(BF16)
    olo = (cother[...] - ohi.astype(F32)).astype(BF16)
    x_ref[0:clusters, :] = ohi
    x_ref[clusters : 2 * clusters, :] = olo

    def out_copy(d):
        return pltpu.make_async_copy(res.at[d], rout_ref.at[lax.rem(i + GROUPS - d, GROUPS)], out_sem.at[d])

    def finish(d, carry):
        p = phi[core * GROUPS + d]
        recon = lax.dot_general(p, chi[...], TN, preferred_element_type=F32)
        recon = recon + lax.dot_general(p, clo[...], TN, preferred_element_type=F32)
        p = pother[d]
        recon = recon + lax.dot_general(p, x_ref[0:clusters, :], TN, preferred_element_type=F32)
        recon = recon + lax.dot_general(p, x_ref[clusters : 2 * clusters, :], TN, preferred_element_type=F32)
        res[d] = rows[core * GROUPS + d].astype(F32) - recon
        out_copy(d).start()
        return carry

    lax.fori_loop(0, GROUPS, finish, 0)
    own_out.wait()
    other_out.wait()

    def drain(d, carry):
        out_copy(d).wait()
        return carry

    lax.fori_loop(0, GROUPS, drain, 0)


def per_device(residuals, codes, counts, centroids):
    nrow, width = residuals.shape
    clusters = centroids.shape[1]
    share = clusters // CHIPS
    blocks = 2 * GROUPS
    dma = pltpu.SemaphoreType.DMA
    quarters = CAP // CHUNK
    scratch = [
        pltpu.VMEM((nrow, width), BF16),
        pltpu.VMEM((clusters, width), F32),
        pltpu.VMEM((GROUPS - 1, CAP, width), BF16),
        pltpu.VMEM((GROUPS - 1, 8, CAP), F32),
        pltpu.VMEM((blocks, CAP, width), BF16),
        pltpu.VMEM((blocks, 8, CAP), F32),
        pltpu.VMEM((blocks, clusters, CAP), F32),
        pltpu.VMEM((blocks, clusters, CAP), BF16),
        pltpu.VMEM((blocks, clusters, CAP), BF16),
        pltpu.VMEM((8, clusters), F32),
        pltpu.VMEM((CHIPS - 1, 8, clusters), F32),
        pltpu.VMEM((clusters, width), F32),
        pltpu.VMEM((CHIPS - 1, share, width), F32),
        pltpu.VMEM((clusters, LANES), F32),
        pltpu.VMEM((CHIPS - 1, share, LANES), F32),
        pltpu.VMEM((clusters, width), F32),
        pltpu.VMEM((clusters, width), BF16),
        pltpu.VMEM((clusters, width), BF16),
        pltpu.VMEM((clusters, LANES), F32),
        pltpu.VMEM((clusters, LANES), F32),
        pltpu.VMEM((GROUPS, clusters, CAP), BF16),
        pltpu.VMEM((clusters, width), F32),
        pltpu.VMEM((GROUPS, CAP, width), F32),
        dma((2,)),
        dma, dma, dma((GROUPS - 1, quarters)), dma((GROUPS - 1,)),
        dma, dma, dma((GROUPS, quarters)), dma((GROUPS,)),
        dma, dma, dma, dma, dma, dma, dma, dma,
        dma, dma, dma, dma, dma((GROUPS,)),
    ]
    cent, resid = pl.pallas_call(
        kernel,
        out_shape=(
            jax.ShapeDtypeStruct(centroids.shape, F32),
            jax.ShapeDtypeStruct((GROUPS, CAP, width), F32),
        ),
        in_specs=[
            pl.BlockSpec(memory_space=pl.ANY),
            pl.BlockSpec(memory_space=pltpu.VMEM),
            pl.BlockSpec(memory_space=pltpu.SMEM),
            pl.BlockSpec(memory_space=pl.ANY),
        ],
        out_specs=(pl.BlockSpec(memory_space=pl.ANY), pl.BlockSpec(memory_space=pl.ANY)),
        scratch_shapes=scratch,
        compiler_params=pltpu.CompilerParams(
            collective_id=0, has_side_effects=True, vmem_limit_bytes=56 * 1024 * 1024
        ),
    )(residuals, codes.reshape(1, nrow), counts.reshape(GROUPS), centroids)
    return cent, resid.reshape(1, 1, GROUPS * CAP, width)


def solution(mesh):
    in_specs = (
        P(("code", "row"), None),
        P(("code", "row")),
        P("code", "row", None),
        P("code", None, None),
    )
    out_specs = (P("code", None, None), P("code", "row", None, None))
    return jax.shard_map(
        per_device, mesh=mesh, in_specs=in_specs, out_specs=out_specs, check_vma=False
    )
```

```python
import jax
import jax.numpy as jnp
from jax import lax
from jax.experimental import pallas as pl
from jax.experimental.pallas import tpu as pltpu
from jax.sharding import PartitionSpec as P

ITERS = 3
SCORE_SCALE = 0.0625
LOG2E = 1.4426950408889634
MESH = pl.DeviceIdType.MESH
GROUPS = 4
CHIPS = 16
SIDE = 4
LANES = 128
CAP = 512
CHUNK = 128
F32 = jnp.float32
BF16 = jnp.bfloat16

NT = (((1,), (1,)), ((), ()))
TN = (((0,), (0,)), ((), ()))


def wait_bytes(ref, sem):
    pltpu.make_async_copy(ref, ref, sem).wait()


def kernel(
    x_hbm, codes_ref, counts_ref, cent_hbm, cent_out, rows_out, p_out,
    x_ref, cent_ref, sendbuf, sendtag, rows, tags, p0, p2, colsend, colrecv, numsend, numrecv,
    masssend, massrecv, call, c2, cn, colacc, massacc,
    in_sem, asend, tsend, arecv, trecv, fsend, ftsend, frecv, ftrecv,
    col_s, col_r, rs_s, rs_r, m_s, m_r, ag_s, ag_r, po_s, po_r, co_s, co_r, rows_sem, p_sem,
):
    i = lax.axis_index("code")
    j = lax.axis_index("row")
    core = lax.rem(j, 2)
    chip = lax.div(j, 2)
    cz = lax.div(chip, SIDE)
    cx = lax.rem(chip, SIDE)
    sib = (i, 2 * chip + 1 - core)
    share = numrecv.shape[1]
    clusters = call.shape[0]
    width = call.shape[1]

    def chip_at(d):
        return lax.rem(cz + lax.div(d, SIDE), SIDE) * SIDE + lax.rem(cx + lax.rem(d, SIDE), SIDE)

    def row_peer(t):
        return (i, 2 * t + core)

    def group(d):
        return lax.rem(i + d, GROUPS)

    def source(d):
        return lax.rem(i + GROUPS - d, GROUPS)

    load_x = pltpu.make_async_copy(x_hbm, x_ref, in_sem.at[0])
    load_x.start()
    load_c = pltpu.make_async_copy(cent_hbm.at[core], cent_ref, in_sem.at[1])
    load_c.start()

    barrier = pltpu.get_barrier_semaphore()
    for d in range(1, GROUPS):
        pl.semaphore_signal(barrier, inc=1, device_id=(group(d), j), device_id_type=MESH)
    pl.semaphore_signal(barrier, inc=1, device_id=sib, device_id_type=MESH)

    def greet(d, carry):
        pl.semaphore_signal(barrier, inc=1, device_id=row_peer(chip_at(d)), device_id_type=MESH)
        return carry

    lax.fori_loop(1, CHIPS, greet, 0)

    load_x.wait()
    half = CAP // 2
    iota_r = lax.broadcasted_iota(jnp.int32, (half, x_ref.shape[0]), 1)
    iota_t = lax.broadcasted_iota(jnp.int32, (half, x_ref.shape[0]), 0)
    diff = iota_r - iota_t
    codes8 = jnp.broadcast_to(codes_ref[...], (8, codes_ref.shape[1]))

    def block(d, h):
        target = group(d)
        start = jnp.int32(0)
        for g in range(GROUPS - 1):
            start = start + jnp.where(g < target, counts_ref[g], 0)
        number = counts_ref[target] - h * half
        pick = jnp.where((diff == start + h * half) & (iota_t < number), 1.0, 0.0).astype(BF16)
        piece = jnp.dot(pick, x_ref[...], preferred_element_type=F32).astype(BF16)
        label = (codes8 - 2 * target + 1).astype(F32).astype(BF16)
        tag = lax.dot_general(label, pick, NT, preferred_element_type=F32)
        return piece, tag

    def a2a_copy(d, q):
        lines = pl.ds(q * CHUNK, CHUNK)
        return pltpu.make_async_remote_copy(
            sendbuf.at[d - 1, lines], rows.at[core * GROUPS + d, lines], asend, arecv.at[d - 1, q],
            device_id=(group(d), j), device_id_type=MESH,
        )

    def tag_copy(d):
        return pltpu.make_async_remote_copy(
            sendtag.at[d - 1], tags.at[core * GROUPS + d], tsend, trecv.at[d - 1],
            device_id=(group(d), j), device_id_type=MESH,
        )

    def forward_copy(d, q):
        lines = pl.ds(q * CHUNK, CHUNK)
        return pltpu.make_async_remote_copy(
            rows.at[core * GROUPS + d, lines], rows.at[core * GROUPS + d, lines], fsend, frecv.at[d, q],
            device_id=sib, device_id_type=MESH,
        )

    def forward_tag(d):
        return pltpu.make_async_remote_copy(
            tags.at[core * GROUPS + d], tags.at[core * GROUPS + d], ftsend, ftrecv.at[d],
            device_id=sib, device_id_type=MESH,
        )

    quarters = CAP // CHUNK
    first = True
    for h in range(2):
        for d in (2, 1, 3):
            piece, tag = block(d, h)
            sendbuf[d - 1, h * half : (h + 1) * half, :] = piece
            sendtag[d - 1, :, h * half : (h + 1) * half] = tag
            if first:
                pl.semaphore_wait(barrier, GROUPS - 1 + 1 + CHIPS - 1)
                first = False
            if h == 1:
                tag_copy(d).start()
            for q in range(quarters // 2):
                a2a_copy(d, h * (quarters // 2) + q).start()
    for h in range(2):
        piece, tag = block(0, h)
        rows[core * GROUPS, h * half : (h + 1) * half, :] = piece
        tags[core * GROUPS, :, h * half : (h + 1) * half] = tag
    forward_tag(0).start()

    def own_forward(q, carry):
        forward_copy(0, q).start()
        return carry

    lax.fori_loop(0, quarters, own_forward, 0)

    def split(c):
        hi = c.astype(BF16)
        c2[0:clusters, :] = hi
        c2[clusters : 2 * clusters, :] = (c - hi.astype(F32)).astype(BF16)
        norm = jnp.sum(c * c, axis=1, keepdims=True) * (SCORE_SCALE * LOG2E)
        cn[...] = jnp.broadcast_to(norm, cn.shape)

    def first_soft(b, lo, n):
        x = rows[b, pl.ds(lo, n), :]
        s = lax.dot_general(c2[...], x, NT, preferred_element_type=F32)
        s = s[0:clusters] + s[clusters : 2 * clusters]
        for k in range(n // LANES):
            at = pl.ds(lo + k * LANES, LANES)
            t = s[:, k * LANES : (k + 1) * LANES] * (2.0 * SCORE_SCALE * LOG2E) - cn[...]
            e = jnp.exp2(t - jnp.max(t, axis=0, keepdims=True))
            total = jnp.sum(e, axis=0, keepdims=True)
            live = tags[b, 0:1, at] == (core + 1).astype(F32)
            p = e * jnp.where(live, 1.0 / total, 0.0)
            p0[b, :, at] = p
            colacc[...] += p

    load_c.wait()
    split(cent_ref[...])
    colacc[...] = jnp.zeros_like(colacc)

    other = 1 - core

    for d in (2, 1, 3):
        tag_copy(d).wait_recv()
        forward_tag(d).start()

    def sib_tag(d, carry):
        forward_tag(d).wait_recv()
        return carry

    lax.fori_loop(0, GROUPS, sib_tag, 0)

    def sib_soft(d, q):
        forward_copy(d, q).wait_recv()
        first_soft(other * GROUPS + d, pl.multiple_of(q * CHUNK, CHUNK), CHUNK)

    def own_soft(q, carry):
        first_soft(core * GROUPS, pl.multiple_of(q * CHUNK, CHUNK), CHUNK)
        sib_soft(0, q)
        return carry

    lax.fori_loop(0, quarters, own_soft, 0)

    def place(t):
        return lax.rem(t, GROUPS - 1) + 1, lax.div(t, GROUPS - 1)

    def arrive(t, carry):
        d, q = place(t)
        a2a_copy(d, q).wait_recv()
        forward_copy(d, q).start()
        first_soft(core * GROUPS + d, pl.multiple_of(q * CHUNK, CHUNK), CHUNK)

        @pl.when(t > 0)
        def _():
            sib_soft(*place(t - 1))

        return carry

    arrivals = quarters * (GROUPS - 1)
    lax.fori_loop(0, arrivals, arrive, 0)

    def rows_copy(d):
        return pltpu.make_async_copy(rows.at[core * GROUPS + d], rows_out.at[source(d)], rows_sem.at[d])

    def p_copy(d):
        return pltpu.make_async_copy(
            p2.at[core * GROUPS + d, pl.ds(0, clusters)], p_out.at[source(d), core], p_sem.at[d]
        )

    def p_forward(d):
        return pltpu.make_async_remote_copy(
            p2.at[other * GROUPS + d, pl.ds(0, clusters)], p_out.at[source(d), core], po_s.at[d], po_r.at[d],
            device_id=sib, device_id_type=MESH,
        )

    def rows_start(d, carry):
        rows_copy(d).start()
        return carry

    lax.fori_loop(0, GROUPS, rows_start, 0)
    sib_soft(GROUPS - 1, quarters - 1)

    def chunk_of(t):
        return pl.ds(pl.multiple_of(t * share, share), share)

    mine = chunk_of(chip)

    def col_copy(d):
        return pltpu.make_async_remote_copy(
            colsend, colrecv.at[d - 1], col_s, col_r, device_id=row_peer(chip_at(d)), device_id_type=MESH
        )

    def rs_copy(d):
        t = chip_at(d)
        return pltpu.make_async_remote_copy(
            numsend.at[chunk_of(t)], numrecv.at[d - 1], rs_s, rs_r, device_id=row_peer(t), device_id_type=MESH
        )

    def mass_copy(d):
        return pltpu.make_async_remote_copy(
            masssend, massrecv.at[d - 1], m_s, m_r, device_id=row_peer(chip_at(d)), device_id_type=MESH
        )

    def ag_copy(d):
        return pltpu.make_async_remote_copy(
            call.at[mine], call.at[mine], ag_s, ag_r, device_id=row_peer(chip_at(d)), device_id_type=MESH
        )

    def each_peer(make):
        def body(d, carry):
            make(d).start()
            return carry

        lax.fori_loop(1, CHIPS, body, 0)

    blocks = 2 * GROUPS
    rest = pl.ds(0, (CHIPS - 1) * share)

    def as_row(parts):
        return jnp.sum(jnp.transpose(parts), axis=0, keepdims=True)

    def as_column(row):
        return jnp.transpose(jnp.broadcast_to(row, (LANES, clusters)))

    def update(step, carry):
        colsend[...] = as_row(colacc[...])
        each_peer(col_copy)
        massacc[...] = jnp.zeros_like(massacc)
        wait_bytes(colrecv, col_r)
        colacc[...] = as_column(1.0 / (colsend[...] + jnp.sum(colrecv[...], axis=0)))

        def weigh(b, carry):
            for k in range(CAP // LANES):
                at = slice(k * LANES, (k + 1) * LANES)
                q = p0[b, :, at] * colacc[...]
                total = jnp.sum(q, axis=0, keepdims=True)
                live = tags[b, 0:1, at] == (core + 1).astype(F32)
                p = q * jnp.where(live, 1.0 / jnp.where(live, total, 1.0), 0.0)
                hi = p.astype(BF16)
                p2[b, 0:clusters, at] = hi
                p2[b, clusters : 2 * clusters, at] = (p - hi.astype(F32)).astype(BF16)
                massacc[...] += p
            part = jnp.dot(p2[b], rows[b], preferred_element_type=F32)
            numsend[...] += part[0:clusters] + part[clusters : 2 * clusters]
            return carry

        numsend[...] = jnp.zeros_like(numsend)
        lax.fori_loop(0, blocks, weigh, 0, unroll=True)
        each_peer(rs_copy)
        masssend[...] = as_row(massacc[...])
        each_peer(mass_copy)

        @pl.when(step == ITERS - 1)
        def _():
            def p_start(d, carry):
                p_copy(d).start()
                p_forward(d).start()
                return carry

            lax.fori_loop(0, GROUPS, p_start, 0)

        wait_bytes(colrecv, col_s)
        wait_bytes(massrecv, m_r)
        massacc[...] = as_column(masssend[...] + jnp.sum(massrecv[...], axis=0))
        wait_bytes(numrecv, rs_r)
        num = numsend[mine, :] + jnp.sum(numrecv[...], axis=0)
        call[mine, :] = num / massacc[mine, 0:1]
        each_peer(ag_copy)
        wait_bytes(massrecv, m_s)
        wait_bytes(numrecv, rs_s)
        wait_bytes(call.at[rest], ag_r)

        @pl.when(step < ITERS - 1)
        def _():
            split(call[...])
            colacc[...] = jnp.zeros_like(colacc)

            def soft(b, carry):
                first_soft(b, 0, CAP)
                return carry

            lax.fori_loop(0, blocks, soft, 0, unroll=True)

        wait_bytes(call.at[rest], ag_s)
        return carry

    lax.fori_loop(0, ITERS, update, 0)

    ccopy = pltpu.make_async_remote_copy(call, cent_out.at[core], co_s, co_r, device_id=sib, device_id_type=MESH)
    ccopy.start()
    own_out = pltpu.make_async_copy(call, cent_out.at[core], in_sem.at[0])
    own_out.start()
    wait_bytes(sendbuf, asend)
    wait_bytes(sendtag, tsend)
    wait_bytes(rows.at[pl.ds(0, GROUPS)], fsend)
    wait_bytes(tags.at[pl.ds(0, GROUPS)], ftsend)

    def drain(d, carry):
        rows_copy(d).wait()
        p_copy(d).wait()
        p_forward(d).wait()
        return carry

    lax.fori_loop(0, GROUPS, drain, 0)
    ccopy.wait()
    own_out.wait()


def finish(p_ref, rows_ref, cent_ref, cout_ref, rout_ref, chi, clo):
    @pl.when(pl.program_id(0) == 0)
    def _():
        c = cent_ref[...]
        hi = c.astype(BF16)
        chi[...] = hi
        clo[...] = (c - hi.astype(F32)).astype(BF16)
        cout_ref[...] = c

    p = p_ref[0]
    recon = lax.dot_general(p, chi[...], TN, preferred_element_type=F32)
    recon = recon + lax.dot_general(p, clo[...], TN, preferred_element_type=F32)
    rout_ref[0] = rows_ref[0].astype(F32) - recon


def per_device(residuals, codes, counts, centroids):
    nrow, width = residuals.shape
    clusters = centroids.shape[1]
    share = clusters // CHIPS
    blocks = 2 * GROUPS
    dma = pltpu.SemaphoreType.DMA
    quarters = CAP // CHUNK
    scratch = [
        pltpu.VMEM((nrow, width), BF16),
        pltpu.VMEM((clusters, width), F32),
        pltpu.VMEM((GROUPS - 1, CAP, width), BF16),
        pltpu.VMEM((GROUPS - 1, 8, CAP), F32),
        pltpu.VMEM((blocks, CAP, width), BF16),
        pltpu.VMEM((blocks, 8, CAP), F32),
        pltpu.VMEM((blocks, clusters, CAP), F32),
        pltpu.VMEM((blocks, 2 * clusters, CAP), BF16),
        pltpu.VMEM((1, clusters), F32),
        pltpu.VMEM((CHIPS - 1, 1, clusters), F32),
        pltpu.VMEM((clusters, width), F32),
        pltpu.VMEM((CHIPS - 1, share, width), F32),
        pltpu.VMEM((1, clusters), F32),
        pltpu.VMEM((CHIPS - 1, 1, clusters), F32),
        pltpu.VMEM((clusters, width), F32),
        pltpu.VMEM((2 * clusters, width), BF16),
        pltpu.VMEM((clusters, LANES), F32),
        pltpu.VMEM((clusters, LANES), F32),
        pltpu.VMEM((clusters, LANES), F32),
        dma((2,)),
        dma, dma, dma((GROUPS - 1, quarters)), dma((GROUPS - 1,)),
        dma, dma, dma((GROUPS, quarters)), dma((GROUPS,)),
        dma, dma, dma, dma, dma, dma, dma, dma,
        dma((GROUPS,)), dma((GROUPS,)), dma, dma,
        dma((GROUPS,)), dma((GROUPS,)),
    ]
    hbm = pl.BlockSpec(memory_space=pl.ANY)
    cent, rows, weights = pl.pallas_call(
        kernel,
        out_shape=(
            jax.ShapeDtypeStruct(centroids.shape, F32),
            jax.ShapeDtypeStruct((GROUPS, CAP, width), BF16),
            jax.ShapeDtypeStruct((GROUPS, 2, clusters, CAP), BF16),
        ),
        in_specs=[hbm, pl.BlockSpec(memory_space=pltpu.VMEM), pl.BlockSpec(memory_space=pltpu.SMEM), hbm],
        out_specs=(hbm, hbm, hbm),
        scratch_shapes=scratch,
        compiler_params=pltpu.CompilerParams(
            collective_id=0, has_side_effects=True, vmem_limit_bytes=56 * 1024 * 1024
        ),
    )(residuals, codes.reshape(1, nrow), counts.reshape(GROUPS), centroids)
    both = 2 * clusters
    cent, resid = pl.pallas_call(
        finish,
        grid=(GROUPS,),
        out_shape=(
            jax.ShapeDtypeStruct((both, width), F32),
            jax.ShapeDtypeStruct((GROUPS, CAP, width), F32),
        ),
        in_specs=[
            pl.BlockSpec((1, both, CAP), lambda s: (s, 0, 0)),
            pl.BlockSpec((1, CAP, width), lambda s: (s, 0, 0)),
            pl.BlockSpec((both, width), lambda s: (0, 0)),
        ],
        out_specs=(
            pl.BlockSpec((both, width), lambda s: (0, 0)),
            pl.BlockSpec((1, CAP, width), lambda s: (s, 0, 0)),
        ),
        scratch_shapes=[pltpu.VMEM((both, width), BF16), pltpu.VMEM((both, width), BF16)],
        compiler_params=pltpu.CompilerParams(vmem_limit_bytes=56 * 1024 * 1024),
    )(weights.reshape(GROUPS, both, CAP), rows, cent.reshape(both, width))
    return cent.reshape(2, clusters, width), resid.reshape(1, 1, GROUPS * CAP, width)


def solution(mesh):
    in_specs = (
        P(("code", "row"), None),
        P(("code", "row")),
        P("code", "row", None),
        P("code", None, None),
    )
    out_specs = (P("code", None, None), P("code", "row", None, None))
    return jax.shard_map(
        per_device, mesh=mesh, in_specs=in_specs, out_specs=out_specs, check_vma=False
    )
```

```python
import jax
import jax.numpy as jnp
from jax import lax
from jax.experimental import pallas as pl
from jax.experimental.pallas import tpu as pltpu
from jax.sharding import PartitionSpec as P

ITERS = 3
SCORE_SCALE = 0.0625
LOG2E = 1.4426950408889634
FULL = 32767.0
MESH = pl.DeviceIdType.MESH
GROUPS = 4
CHIPS = 16
SIDE = 4
LANES = 128
CAP = 512
CHUNK = 128
TILE = 512
F32 = jnp.float32
BF16 = jnp.bfloat16

NT = (((1,), (1,)), ((), ()))
TN = (((0,), (0,)), ((), ()))


def wait_bytes(ref, sem):
    pltpu.make_async_copy(ref, ref, sem).wait()


def kernel(
    x_hbm, codes_ref, counts_ref, cent_hbm, cent_out, rows_out, p_out,
    x_ref, cent_ref, sendbuf, sendtag, rows, tags, p0, p2, colsend, colrecv, numsend, codesend, numrecv,
    masssend, massrecv, call, callcode, scalesend, scalerecv, c2, cn, colacc, massacc,
    in_sem, asend, tsend, arecv, trecv, fsend, ftsend, frecv, ftrecv,
    col_s, col_r, rs_s, rs_r, m_s, m_r, ag_s, ag_r, sc_s, sc_r, po_s, po_r, co_s, co_r, rows_sem, p_sem,
):
    i = lax.axis_index("code")
    j = lax.axis_index("row")
    core = lax.rem(j, 2)
    chip = lax.div(j, 2)
    cz = lax.div(chip, SIDE)
    cx = lax.rem(chip, SIDE)
    sib = (i, 2 * chip + 1 - core)
    share = numrecv.shape[1]
    clusters = call.shape[0]
    width = call.shape[1]

    def chip_at(d):
        return lax.rem(cz + lax.div(d, SIDE), SIDE) * SIDE + lax.rem(cx + lax.rem(d, SIDE), SIDE)

    def row_peer(t):
        return (i, 2 * t + core)

    def group(d):
        return lax.rem(i + d, GROUPS)

    def source(d):
        return lax.rem(i + GROUPS - d, GROUPS)

    load_x = pltpu.make_async_copy(x_hbm, x_ref, in_sem.at[0])
    load_x.start()
    load_c = pltpu.make_async_copy(cent_hbm.at[core], cent_ref, in_sem.at[1])
    load_c.start()

    barrier = pltpu.get_barrier_semaphore()
    for d in range(1, GROUPS):
        pl.semaphore_signal(barrier, inc=1, device_id=(group(d), j), device_id_type=MESH)
    pl.semaphore_signal(barrier, inc=1, device_id=sib, device_id_type=MESH)

    def greet(d, carry):
        pl.semaphore_signal(barrier, inc=1, device_id=row_peer(chip_at(d)), device_id_type=MESH)
        return carry

    lax.fori_loop(1, CHIPS, greet, 0)

    load_x.wait()
    half = CAP // 2
    iota_r = lax.broadcasted_iota(jnp.int32, (half, x_ref.shape[0]), 1)
    iota_t = lax.broadcasted_iota(jnp.int32, (half, x_ref.shape[0]), 0)
    diff = iota_r - iota_t
    codes8 = jnp.broadcast_to(codes_ref[...], (8, codes_ref.shape[1]))

    def block(d, h):
        target = group(d)
        start = jnp.int32(0)
        for g in range(GROUPS - 1):
            start = start + jnp.where(g < target, counts_ref[g], 0)
        number = counts_ref[target] - h * half
        pick = jnp.where((diff == start + h * half) & (iota_t < number), 1.0, 0.0).astype(BF16)
        piece = jnp.dot(pick, x_ref[...], preferred_element_type=F32).astype(BF16)
        label = (codes8 - 2 * target + 1).astype(F32).astype(BF16)
        tag = lax.dot_general(label, pick, NT, preferred_element_type=F32)
        return piece, tag

    def a2a_copy(d, q):
        lines = pl.ds(q * CHUNK, CHUNK)
        return pltpu.make_async_remote_copy(
            sendbuf.at[d - 1, lines], rows.at[core * GROUPS + d, lines], asend, arecv.at[d - 1, q],
            device_id=(group(d), j), device_id_type=MESH,
        )

    def tag_copy(d):
        return pltpu.make_async_remote_copy(
            sendtag.at[d - 1], tags.at[core * GROUPS + d], tsend, trecv.at[d - 1],
            device_id=(group(d), j), device_id_type=MESH,
        )

    def forward_copy(d, q):
        lines = pl.ds(q * CHUNK, CHUNK)
        return pltpu.make_async_remote_copy(
            rows.at[core * GROUPS + d, lines], rows.at[core * GROUPS + d, lines], fsend, frecv.at[d, q],
            device_id=sib, device_id_type=MESH,
        )

    def forward_tag(d):
        return pltpu.make_async_remote_copy(
            tags.at[core * GROUPS + d], tags.at[core * GROUPS + d], ftsend, ftrecv.at[d],
            device_id=sib, device_id_type=MESH,
        )

    quarters = CAP // CHUNK
    first = True
    for h in range(2):
        for d in (2, 1, 3):
            piece, tag = block(d, h)
            sendbuf[d - 1, h * half : (h + 1) * half, :] = piece
            sendtag[d - 1, :, h * half : (h + 1) * half] = tag
            if first:
                pl.semaphore_wait(barrier, GROUPS - 1 + 1 + CHIPS - 1)
                first = False
            if h == 1:
                tag_copy(d).start()
            for q in range(quarters // 2):
                a2a_copy(d, h * (quarters // 2) + q).start()
    for h in range(2):
        piece, tag = block(0, h)
        rows[core * GROUPS, h * half : (h + 1) * half, :] = piece
        tags[core * GROUPS, :, h * half : (h + 1) * half] = tag
    forward_tag(0).start()

    def own_forward(q, carry):
        forward_copy(0, q).start()
        return carry

    lax.fori_loop(0, quarters, own_forward, 0)

    def split(c):
        hi = c.astype(BF16)
        c2[0:clusters, :] = hi
        c2[clusters : 2 * clusters, :] = (c - hi.astype(F32)).astype(BF16)
        norm = jnp.sum(c * c, axis=1, keepdims=True) * (SCORE_SCALE * LOG2E)
        cn[...] = jnp.broadcast_to(norm, cn.shape)

    def first_soft(parts, n):
        x = [rows[b, pl.ds(lo, n), :] for b, lo in parts]
        x = x[0] if len(x) == 1 else jnp.concatenate(x, axis=0)
        s = lax.dot_general(c2[...], x, NT, preferred_element_type=F32)
        s = s[0:clusters] + s[clusters : 2 * clusters]
        for m, (b, lo) in enumerate(parts):
            for k in range(n // LANES):
                at = pl.ds(lo + k * LANES, LANES)
                first = m * n + k * LANES
                t = s[:, first : first + LANES] * (2.0 * SCORE_SCALE * LOG2E) - cn[...]
                e = jnp.exp2(t - jnp.max(t, axis=0, keepdims=True))
                total = jnp.sum(e, axis=0, keepdims=True)
                live = tags[b, 0:1, at] == (core + 1).astype(F32)
                p = e * jnp.where(live, 1.0 / total, 0.0)
                p0[b, :, at] = p
                colacc[...] += p

    load_c.wait()
    split(cent_ref[...])
    colacc[...] = jnp.zeros_like(colacc)

    other = 1 - core

    first_soft([(core * GROUPS, 0)], CAP)
    forward_tag(0).wait_recv()

    def sib_wait(q, carry):
        forward_copy(0, q).wait_recv()
        return carry

    lax.fori_loop(0, quarters, sib_wait, 0)
    first_soft([(other * GROUPS, 0)], CAP)

    for d in (2, 1, 3):
        tag_copy(d).wait_recv()
        forward_tag(d).start()

    def sib_tag(d, carry):
        forward_tag(d).wait_recv()
        return carry

    lax.fori_loop(1, GROUPS, sib_tag, 0)

    for q in range(quarters):
        for d in (1, 3, 2):
            a2a_copy(d, q).wait_recv()
            forward_copy(d, q).start()
        if q == 0:
            first_soft([(core * GROUPS + d, 0) for d in (1, 3, 2)], CHUNK)
            continue
        for d in (1, 3, 2):
            forward_copy(d, q - 1).wait_recv()
        for d in (1, 3, 2):
            first_soft([(core * GROUPS + d, q * CHUNK), (other * GROUPS + d, (q - 1) * CHUNK)], CHUNK)

    def rows_copy(d):
        return pltpu.make_async_copy(rows.at[core * GROUPS + d], rows_out.at[source(d)], rows_sem.at[d])

    def p_copy(d):
        return pltpu.make_async_copy(
            p2.at[core * GROUPS + d, pl.ds(0, clusters)], p_out.at[source(d), core], p_sem.at[d]
        )

    def p_forward(d):
        return pltpu.make_async_remote_copy(
            p2.at[other * GROUPS + d, pl.ds(0, clusters)], p_out.at[source(d), core], po_s.at[d], po_r.at[d],
            device_id=sib, device_id_type=MESH,
        )

    def rows_start(d, carry):
        rows_copy(d).start()
        return carry

    lax.fori_loop(0, GROUPS, rows_start, 0)
    for d in (1, 3, 2):
        forward_copy(d, quarters - 1).wait_recv()
    first_soft([(other * GROUPS + d, (quarters - 1) * CHUNK) for d in (1, 3, 2)], CHUNK)

    def chunk_of(t):
        return pl.ds(pl.multiple_of(t * share, share), share)

    mine = chunk_of(chip)

    def col_copy(d):
        return pltpu.make_async_remote_copy(
            colsend, colrecv.at[d - 1], col_s, col_r, device_id=row_peer(chip_at(d)), device_id_type=MESH
        )

    def rs_copy(d):
        t = chip_at(d)
        return pltpu.make_async_remote_copy(
            codesend.at[chunk_of(t)], numrecv.at[d - 1], rs_s, rs_r, device_id=row_peer(t), device_id_type=MESH
        )

    def mass_copy(d):
        return pltpu.make_async_remote_copy(
            masssend, massrecv.at[d - 1], m_s, m_r, device_id=row_peer(chip_at(d)), device_id_type=MESH
        )

    def ag_copy(d):
        return pltpu.make_async_remote_copy(
            callcode.at[mine], callcode.at[mine], ag_s, ag_r, device_id=row_peer(chip_at(d)), device_id_type=MESH
        )

    def scale_copy(d):
        return pltpu.make_async_remote_copy(
            scalesend, scalerecv.at[d - 1], sc_s, sc_r, device_id=row_peer(chip_at(d)), device_id_type=MESH
        )

    def encode(v):
        top = jnp.maximum(jnp.max(jnp.abs(v), axis=1, keepdims=True), 1e-34)
        return jnp.round(v * (FULL / top)).astype(jnp.int32).astype(jnp.int16), top * (1.0 / FULL)

    def decode(code, scale):
        return code.astype(jnp.int32).astype(F32) * scale

    def each_peer(make):
        def body(d, carry):
            make(d).start()
            return carry

        lax.fori_loop(1, CHIPS, body, 0)

    blocks = 2 * GROUPS
    rest = pl.ds(0, (CHIPS - 1) * share)

    def as_row(parts):
        return jnp.sum(jnp.transpose(parts), axis=0, keepdims=True)

    def as_column(row):
        return jnp.transpose(jnp.broadcast_to(row, (LANES, clusters)))

    def update(step, carry):
        colsend[...] = as_row(colacc[...])
        each_peer(col_copy)
        massacc[...] = jnp.zeros_like(massacc)
        wait_bytes(colrecv, col_r)
        colacc[...] = as_column(1.0 / (colsend[...] + jnp.sum(colrecv[...], axis=0)))

        def weigh(b, carry):
            for k in range(CAP // LANES):
                at = slice(k * LANES, (k + 1) * LANES)
                q = p0[b, :, at] * colacc[...]
                total = jnp.sum(q, axis=0, keepdims=True)
                live = tags[b, 0:1, at] == (core + 1).astype(F32)
                p = q * jnp.where(live, 1.0 / jnp.where(live, total, 1.0), 0.0)
                hi = p.astype(BF16)
                p2[b, 0:clusters, at] = hi
                p2[b, clusters : 2 * clusters, at] = (p - hi.astype(F32)).astype(BF16)
                massacc[...] += p
            part = jnp.dot(p2[b], rows[b], preferred_element_type=F32)
            numsend[...] += part[0:clusters] + part[clusters : 2 * clusters]
            return carry

        numsend[...] = jnp.zeros_like(numsend)
        lax.fori_loop(0, blocks, weigh, 0, unroll=True)
        code, scale = encode(numsend[...])
        codesend[...] = code
        each_peer(rs_copy)
        masssend[0:1, :] = as_row(massacc[...])
        masssend[1:2, :] = jnp.transpose(jnp.broadcast_to(scale, (clusters, LANES)))[0:1, :]
        each_peer(mass_copy)
        massrecv[CHIPS - 1] = masssend[...]

        @pl.when(step == ITERS - 1)
        def _():
            def p_start(d, carry):
                p_copy(d).start()
                p_forward(d).start()
                return carry

            lax.fori_loop(0, GROUPS, p_start, 0)

        wait_bytes(colrecv, col_s)
        wait_bytes(massrecv.at[pl.ds(0, CHIPS - 1)], m_r)
        massacc[...] = as_column(jnp.sum(massrecv[:, 0:1, :], axis=0))
        scales = jnp.concatenate(
            [massrecv[:, 1, :], jnp.zeros((LANES - CHIPS, clusters), F32)], axis=0
        )
        colacc[...] = jnp.transpose(scales)
        wait_bytes(numrecv, rs_r)
        num = numsend[mine, :]
        for d in range(CHIPS - 1):
            num = num + decode(numrecv[d], colacc[mine, d : d + 1])
        code, scale = encode(num / massacc[mine, 0:1])
        callcode[mine, :] = code
        each_peer(ag_copy)
        massacc[...] = jnp.zeros_like(massacc)
        massacc[mine, :] = jnp.broadcast_to(scale, (share, LANES))
        scalesend[...] = jnp.transpose(massacc[...])[0:1, :]
        each_peer(scale_copy)
        wait_bytes(massrecv.at[pl.ds(0, CHIPS - 1)], m_s)
        wait_bytes(numrecv, rs_s)
        wait_bytes(scalerecv, sc_r)
        colacc[...] = as_column(scalesend[...] + jnp.sum(scalerecv[...], axis=0))
        wait_bytes(callcode.at[rest], ag_r)
        call[...] = decode(callcode[...], colacc[:, 0:1])

        @pl.when(step < ITERS - 1)
        def _():
            split(call[...])
            colacc[...] = jnp.zeros_like(colacc)

            def soft(b, carry):
                first_soft([(b, 0)], CAP)
                return carry

            lax.fori_loop(0, blocks, soft, 0, unroll=True)

        wait_bytes(callcode.at[rest], ag_s)
        wait_bytes(scalerecv, sc_s)
        return carry

    lax.fori_loop(0, ITERS, update, 0)

    ccopy = pltpu.make_async_remote_copy(call, cent_out.at[core], co_s, co_r, device_id=sib, device_id_type=MESH)
    ccopy.start()
    own_out = pltpu.make_async_copy(call, cent_out.at[core], in_sem.at[0])
    own_out.start()
    wait_bytes(sendbuf, asend)
    wait_bytes(sendtag, tsend)
    wait_bytes(rows.at[pl.ds(0, GROUPS)], fsend)
    wait_bytes(tags.at[pl.ds(0, GROUPS)], ftsend)

    def drain(d, carry):
        rows_copy(d).wait()
        p_copy(d).wait()
        p_forward(d).wait()
        return carry

    lax.fori_loop(0, GROUPS, drain, 0)
    ccopy.wait()
    own_out.wait()


def finish(p_ref, rows_ref, cent_ref, cout_ref, rout_ref, chi, clo):
    @pl.when((pl.program_id(0) == 0) & (pl.program_id(1) == 0))
    def _():
        c = cent_ref[...]
        hi = c.astype(BF16)
        chi[...] = hi
        clo[...] = (c - hi.astype(F32)).astype(BF16)
        cout_ref[...] = c

    p = p_ref[0]
    recon = lax.dot_general(p, chi[...], TN, preferred_element_type=F32)
    recon = recon + lax.dot_general(p, clo[...], TN, preferred_element_type=F32)
    rout_ref[0] = rows_ref[0].astype(F32) - recon


def per_device(residuals, codes, counts, centroids):
    nrow, width = residuals.shape
    clusters = centroids.shape[1]
    share = clusters // CHIPS
    blocks = 2 * GROUPS
    dma = pltpu.SemaphoreType.DMA
    quarters = CAP // CHUNK
    scratch = [
        pltpu.VMEM((nrow, width), BF16),
        pltpu.VMEM((clusters, width), F32),
        pltpu.VMEM((GROUPS - 1, CAP, width), BF16),
        pltpu.VMEM((GROUPS - 1, 8, CAP), F32),
        pltpu.VMEM((blocks, CAP, width), BF16),
        pltpu.VMEM((blocks, 8, CAP), F32),
        pltpu.VMEM((blocks, clusters, CAP), F32),
        pltpu.VMEM((blocks, 2 * clusters, CAP), BF16),
        pltpu.VMEM((1, clusters), F32),
        pltpu.VMEM((CHIPS - 1, 1, clusters), F32),
        pltpu.VMEM((clusters, width), F32),
        pltpu.VMEM((clusters, width), jnp.int16),
        pltpu.VMEM((CHIPS - 1, share, width), jnp.int16),
        pltpu.VMEM((2, clusters), F32),
        pltpu.VMEM((CHIPS, 2, clusters), F32),
        pltpu.VMEM((clusters, width), F32),
        pltpu.VMEM((clusters, width), jnp.int16),
        pltpu.VMEM((1, clusters), F32),
        pltpu.VMEM((CHIPS - 1, 1, clusters), F32),
        pltpu.VMEM((2 * clusters, width), BF16),
        pltpu.VMEM((clusters, LANES), F32),
        pltpu.VMEM((clusters, LANES), F32),
        pltpu.VMEM((clusters, LANES), F32),
        dma((2,)),
        dma, dma, dma((GROUPS - 1, quarters)), dma((GROUPS - 1,)),
        dma, dma, dma((GROUPS, quarters)), dma((GROUPS,)),
        dma, dma, dma, dma, dma, dma, dma, dma, dma, dma,
        dma((GROUPS,)), dma((GROUPS,)), dma, dma,
        dma((GROUPS,)), dma((GROUPS,)),
    ]
    hbm = pl.BlockSpec(memory_space=pl.ANY)
    cent, rows, weights = pl.pallas_call(
        kernel,
        out_shape=(
            jax.ShapeDtypeStruct(centroids.shape, F32),
            jax.ShapeDtypeStruct((GROUPS, CAP, width), BF16),
            jax.ShapeDtypeStruct((GROUPS, 2, clusters, CAP), BF16),
        ),
        in_specs=[hbm, pl.BlockSpec(memory_space=pltpu.VMEM), pl.BlockSpec(memory_space=pltpu.SMEM), hbm],
        out_specs=(hbm, hbm, hbm),
        scratch_shapes=scratch,
        compiler_params=pltpu.CompilerParams(
            collective_id=0, has_side_effects=True, vmem_limit_bytes=56 * 1024 * 1024
        ),
    )(residuals, codes.reshape(1, nrow), counts.reshape(GROUPS), centroids)
    both = 2 * clusters
    cent, resid = pl.pallas_call(
        finish,
        grid=(GROUPS, CAP // TILE),
        out_shape=(
            jax.ShapeDtypeStruct((both, width), F32),
            jax.ShapeDtypeStruct((GROUPS, CAP, width), F32),
        ),
        in_specs=[
            pl.BlockSpec((1, both, TILE), lambda s, t: (s, 0, t)),
            pl.BlockSpec((1, TILE, width), lambda s, t: (s, t, 0)),
            pl.BlockSpec((both, width), lambda s, t: (0, 0)),
        ],
        out_specs=(
            pl.BlockSpec((both, width), lambda s, t: (0, 0)),
            pl.BlockSpec((1, TILE, width), lambda s, t: (s, t, 0)),
        ),
        scratch_shapes=[pltpu.VMEM((both, width), BF16), pltpu.VMEM((both, width), BF16)],
        compiler_params=pltpu.CompilerParams(vmem_limit_bytes=56 * 1024 * 1024),
    )(weights.reshape(GROUPS, both, CAP), rows, cent.reshape(both, width))
    return cent.reshape(2, clusters, width), resid.reshape(1, 1, GROUPS * CAP, width)


def solution(mesh):
    in_specs = (
        P(("code", "row"), None),
        P(("code", "row")),
        P("code", "row", None),
        P("code", None, None),
    )
    out_specs = (P("code", None, None), P("code", "row", None, None))
    return jax.shard_map(
        per_device, mesh=mesh, in_specs=in_specs, out_specs=out_specs, check_vma=False
    )
```

```python
import jax
import jax.numpy as jnp
from jax import lax
from jax.experimental import pallas as pl
from jax.experimental.pallas import tpu as pltpu
from jax.sharding import PartitionSpec as P

ITERS = 3
SCORE_SCALE = 0.0625
LOG2E = 1.4426950408889634
FULL = 32767.0
MESH = pl.DeviceIdType.MESH
GROUPS = 4
CHIPS = 16
SIDE = 4
FAR_FIRST = sorted(
    [(z, x) for z in range(SIDE) for x in range(SIDE) if z or x],
    key=lambda s: -min(s[0], SIDE - s[0]) - min(s[1], SIDE - s[1]),
)
LANES = 128
CAP = 512
CHUNK = 128
F32 = jnp.float32
BF16 = jnp.bfloat16

NT = (((1,), (1,)), ((), ()))
TN = (((0,), (0,)), ((), ()))


def wait_bytes(ref, sem):
    pltpu.make_async_copy(ref, ref, sem).wait()


def kernel(
    x_hbm, codes_ref, counts_ref, cent_hbm, cent_out, rows_out, p_out,
    x_ref, cent_ref, sendbuf, sendtag, rows, tags, p0, p2, colsend, colrecv, numsend, codesend, numrecv,
    masssend, massrecv, call, callcode, scalesend, scalerecv, c2, cn, colacc, massacc,
    in_sem, asend, tsend, arecv, trecv, fsend, ftsend, frecv, ftrecv,
    col_s, col_r, rs_s, rs_r, m_s, m_r, ag_s, ag_r, sc_s, sc_r, po_s, po_r, co_s, co_r, rows_sem, p_sem,
):
    i = lax.axis_index("code")
    j = lax.axis_index("row")
    core = lax.rem(j, 2)
    chip = lax.div(j, 2)
    cz = lax.div(chip, SIDE)
    cx = lax.rem(chip, SIDE)
    sib = (i, 2 * chip + 1 - core)
    share = numrecv.shape[1]
    clusters = call.shape[0]
    width = call.shape[1]

    peers = [lax.rem(cz + dz, SIDE) * SIDE + lax.rem(cx + dx, SIDE) for dz, dx in FAR_FIRST]

    def chip_at(d):
        return peers[d - 1]

    def row_peer(t):
        return (i, 2 * t + core)

    def group(d):
        return lax.rem(i + d, GROUPS)

    def source(d):
        return lax.rem(i + GROUPS - d, GROUPS)

    load_x = pltpu.make_async_copy(x_hbm, x_ref, in_sem.at[0])
    load_x.start()
    load_c = pltpu.make_async_copy(cent_hbm.at[core], cent_ref, in_sem.at[1])
    load_c.start()

    barrier = pltpu.get_barrier_semaphore()
    for d in range(1, GROUPS):
        pl.semaphore_signal(barrier, inc=1, device_id=(group(d), j), device_id_type=MESH)
    pl.semaphore_signal(barrier, inc=1, device_id=sib, device_id_type=MESH)

    for d in range(1, CHIPS):
        pl.semaphore_signal(barrier, inc=1, device_id=row_peer(chip_at(d)), device_id_type=MESH)

    load_x.wait()
    half = CAP // 2
    iota_r = lax.broadcasted_iota(jnp.int32, (half, x_ref.shape[0]), 1)
    iota_t = lax.broadcasted_iota(jnp.int32, (half, x_ref.shape[0]), 0)
    diff = iota_r - iota_t
    codes8 = jnp.broadcast_to(codes_ref[...], (8, codes_ref.shape[1]))

    def block(d, h):
        target = group(d)
        start = jnp.int32(0)
        for g in range(GROUPS - 1):
            start = start + jnp.where(g < target, counts_ref[g], 0)
        number = counts_ref[target] - h * half
        pick = jnp.where((diff == start + h * half) & (iota_t < number), 1.0, 0.0).astype(BF16)
        piece = jnp.dot(pick, x_ref[...], preferred_element_type=F32).astype(BF16)
        label = (codes8 - 2 * target + 1).astype(F32).astype(BF16)
        tag = lax.dot_general(label, pick, NT, preferred_element_type=F32)
        return piece, tag

    def a2a_copy(d, q):
        lines = pl.ds(q * CHUNK, CHUNK)
        return pltpu.make_async_remote_copy(
            sendbuf.at[d - 1, lines], rows.at[core * GROUPS + d, lines], asend, arecv.at[d - 1, q],
            device_id=(group(d), j), device_id_type=MESH,
        )

    def tag_copy(d):
        return pltpu.make_async_remote_copy(
            sendtag.at[d - 1], tags.at[core * GROUPS + d], tsend, trecv.at[d - 1],
            device_id=(group(d), j), device_id_type=MESH,
        )

    def forward_copy(d, q):
        lines = pl.ds(q * CHUNK, CHUNK)
        return pltpu.make_async_remote_copy(
            rows.at[core * GROUPS + d, lines], rows.at[core * GROUPS + d, lines], fsend, frecv.at[d, q],
            device_id=sib, device_id_type=MESH,
        )

    def forward_tag(d):
        return pltpu.make_async_remote_copy(
            tags.at[core * GROUPS + d], tags.at[core * GROUPS + d], ftsend, ftrecv.at[d],
            device_id=sib, device_id_type=MESH,
        )

    quarters = CAP // CHUNK
    first = True
    for h in range(2):
        for d in (2, 1, 3):
            piece, tag = block(d, h)
            sendbuf[d - 1, h * half : (h + 1) * half, :] = piece
            sendtag[d - 1, :, h * half : (h + 1) * half] = tag
            if first:
                pl.semaphore_wait(barrier, GROUPS - 1 + 1 + CHIPS - 1)
                first = False
            if h == 1:
                tag_copy(d).start()
            for q in range(quarters // 2):
                a2a_copy(d, h * (quarters // 2) + q).start()
    for h in range(2):
        piece, tag = block(0, h)
        rows[core * GROUPS, h * half : (h + 1) * half, :] = piece
        tags[core * GROUPS, :, h * half : (h + 1) * half] = tag
    forward_tag(0).start()

    def own_forward(q, carry):
        forward_copy(0, q).start()
        return carry

    lax.fori_loop(0, quarters, own_forward, 0)

    def split(c):
        hi = c.astype(BF16)
        c2[0:clusters, :] = hi
        c2[clusters : 2 * clusters, :] = (c - hi.astype(F32)).astype(BF16)
        norm = jnp.sum(c * c, axis=1, keepdims=True) * (SCORE_SCALE * LOG2E)
        cn[...] = jnp.broadcast_to(norm, cn.shape)

    def first_soft(parts, n):
        x = [rows[b, pl.ds(lo, n), :] for b, lo in parts]
        x = x[0] if len(x) == 1 else jnp.concatenate(x, axis=0)
        s = lax.dot_general(c2[...], x, NT, preferred_element_type=F32)
        s = s[0:clusters] + s[clusters : 2 * clusters]
        for m, (b, lo) in enumerate(parts):
            for k in range(n // LANES):
                at = pl.ds(lo + k * LANES, LANES)
                first = m * n + k * LANES
                t = s[:, first : first + LANES] * (2.0 * SCORE_SCALE * LOG2E) - cn[...]
                e = jnp.exp2(t - jnp.max(t, axis=0, keepdims=True))
                total = jnp.sum(e, axis=0, keepdims=True)
                live = tags[b, 0:1, at] == (core + 1).astype(F32)
                p = e * jnp.where(live, 1.0 / total, 0.0)
                p0[b, :, at] = p
                colacc[...] += p

    load_c.wait()
    split(cent_ref[...])
    colacc[...] = jnp.zeros_like(colacc)

    other = 1 - core

    first_soft([(core * GROUPS, 0)], CAP)
    forward_tag(0).wait_recv()

    def sib_wait(q, carry):
        forward_copy(0, q).wait_recv()
        return carry

    lax.fori_loop(0, quarters, sib_wait, 0)
    first_soft([(other * GROUPS, 0)], CAP)

    for d in (2, 1, 3):
        tag_copy(d).wait_recv()
        forward_tag(d).start()

    def sib_tag(d, carry):
        forward_tag(d).wait_recv()
        return carry

    lax.fori_loop(1, GROUPS, sib_tag, 0)

    for q in range(quarters):
        for d in (1, 3, 2):
            a2a_copy(d, q).wait_recv()
            forward_copy(d, q).start()
        if q == 0:
            first_soft([(core * GROUPS + d, 0) for d in (1, 3, 2)], CHUNK)
            continue
        for d in (1, 3, 2):
            forward_copy(d, q - 1).wait_recv()
        for d in (1, 3, 2):
            first_soft([(core * GROUPS + d, q * CHUNK), (other * GROUPS + d, (q - 1) * CHUNK)], CHUNK)

    def rows_copy(d):
        return pltpu.make_async_copy(rows.at[core * GROUPS + d], rows_out.at[source(d)], rows_sem.at[d])

    def p_copy(d):
        return pltpu.make_async_copy(
            p2.at[core * GROUPS + d, pl.ds(0, clusters)], p_out.at[source(d), core], p_sem.at[d]
        )

    def p_forward(d):
        return pltpu.make_async_remote_copy(
            p2.at[other * GROUPS + d, pl.ds(0, clusters)], p_out.at[source(d), core], po_s.at[d], po_r.at[d],
            device_id=sib, device_id_type=MESH,
        )

    def rows_start(d, carry):
        rows_copy(d).start()
        return carry

    lax.fori_loop(0, GROUPS, rows_start, 0)
    for d in (1, 3, 2):
        forward_copy(d, quarters - 1).wait_recv()
    first_soft([(other * GROUPS + d, (quarters - 1) * CHUNK) for d in (1, 3, 2)], CHUNK)

    def chunk_of(t):
        return pl.ds(pl.multiple_of(t * share, share), share)

    mine = chunk_of(chip)

    def col_copy(d):
        return pltpu.make_async_remote_copy(
            colsend, colrecv.at[d - 1], col_s, col_r, device_id=row_peer(chip_at(d)), device_id_type=MESH
        )

    def rs_copy(d):
        t = chip_at(d)
        return pltpu.make_async_remote_copy(
            codesend.at[chunk_of(t)], numrecv.at[d - 1], rs_s, rs_r, device_id=row_peer(t), device_id_type=MESH
        )

    def mass_copy(d):
        return pltpu.make_async_remote_copy(
            masssend, massrecv.at[d - 1], m_s, m_r, device_id=row_peer(chip_at(d)), device_id_type=MESH
        )

    def ag_copy(d):
        return pltpu.make_async_remote_copy(
            callcode.at[mine], callcode.at[mine], ag_s, ag_r, device_id=row_peer(chip_at(d)), device_id_type=MESH
        )

    def scale_copy(d):
        return pltpu.make_async_remote_copy(
            scalesend, scalerecv.at[d - 1], sc_s, sc_r, device_id=row_peer(chip_at(d)), device_id_type=MESH
        )

    def encode(v):
        top = jnp.maximum(jnp.max(jnp.abs(v), axis=1, keepdims=True), 1e-34)
        return jnp.round(v * (FULL / top)).astype(jnp.int32).astype(jnp.int16), top * (1.0 / FULL)

    def decode(code, scale):
        return code.astype(jnp.int32).astype(F32) * scale

    def each_peer(make):
        for d in range(1, CHIPS):
            make(d).start()

    blocks = 2 * GROUPS
    rest = pl.ds(0, (CHIPS - 1) * share)

    def as_row(parts):
        return jnp.sum(jnp.transpose(parts), axis=0, keepdims=True)

    def as_column(row):
        return jnp.transpose(jnp.broadcast_to(row, (LANES, clusters)))

    def update(step, carry):
        colsend[...] = as_row(colacc[...])
        each_peer(col_copy)
        massacc[...] = jnp.zeros_like(massacc)
        wait_bytes(colrecv, col_r)
        colacc[...] = as_column(1.0 / (colsend[...] + jnp.sum(colrecv[...], axis=0)))

        def weigh(b, carry):
            for k in range(CAP // LANES):
                at = slice(k * LANES, (k + 1) * LANES)
                q = p0[b, :, at] * colacc[...]
                total = jnp.sum(q, axis=0, keepdims=True)
                live = tags[b, 0:1, at] == (core + 1).astype(F32)
                p = q * jnp.where(live, 1.0 / jnp.where(live, total, 1.0), 0.0)
                hi = p.astype(BF16)
                p2[b, 0:clusters, at] = hi
                p2[b, clusters : 2 * clusters, at] = (p - hi.astype(F32)).astype(BF16)
                massacc[...] += p
            part = jnp.dot(p2[b], rows[b], preferred_element_type=F32)
            numsend[...] += part[0:clusters] + part[clusters : 2 * clusters]
            return carry

        numsend[...] = jnp.zeros_like(numsend)
        lax.fori_loop(0, blocks, weigh, 0, unroll=True)
        code, scale = encode(numsend[...])
        codesend[...] = code
        each_peer(rs_copy)
        masssend[0:1, :] = as_row(massacc[...])
        masssend[1:2, :] = jnp.transpose(jnp.broadcast_to(scale, (clusters, LANES)))[0:1, :]
        each_peer(mass_copy)
        massrecv[CHIPS - 1] = masssend[...]

        @pl.when(step == ITERS - 1)
        def _():
            def p_start(d, carry):
                p_copy(d).start()
                p_forward(d).start()
                return carry

            lax.fori_loop(0, GROUPS, p_start, 0)

        wait_bytes(colrecv, col_s)
        wait_bytes(massrecv.at[pl.ds(0, CHIPS - 1)], m_r)
        massacc[...] = as_column(jnp.sum(massrecv[:, 0:1, :], axis=0))
        scales = jnp.concatenate(
            [massrecv[:, 1, :], jnp.zeros((LANES - CHIPS, clusters), F32)], axis=0
        )
        colacc[...] = jnp.transpose(scales)
        wait_bytes(numrecv, rs_r)
        num = numsend[mine, :]
        for d in range(CHIPS - 1):
            num = num + decode(numrecv[d], colacc[mine, d : d + 1])
        code, scale = encode(num / massacc[mine, 0:1])
        callcode[mine, :] = code
        each_peer(ag_copy)
        massacc[...] = jnp.zeros_like(massacc)
        massacc[mine, :] = jnp.broadcast_to(scale, (share, LANES))
        scalesend[...] = jnp.transpose(massacc[...])[0:1, :]
        each_peer(scale_copy)
        wait_bytes(massrecv.at[pl.ds(0, CHIPS - 1)], m_s)
        wait_bytes(numrecv, rs_s)
        wait_bytes(scalerecv, sc_r)
        colacc[...] = as_column(scalesend[...] + jnp.sum(scalerecv[...], axis=0))
        wait_bytes(callcode.at[rest], ag_r)
        call[...] = decode(callcode[...], colacc[:, 0:1])

        @pl.when(step < ITERS - 1)
        def _():
            split(call[...])
            colacc[...] = jnp.zeros_like(colacc)

            def soft(b, carry):
                first_soft([(b, 0)], CAP)
                return carry

            lax.fori_loop(0, blocks, soft, 0, unroll=True)

        wait_bytes(callcode.at[rest], ag_s)
        wait_bytes(scalerecv, sc_s)
        return carry

    lax.fori_loop(0, ITERS, update, 0)

    ccopy = pltpu.make_async_remote_copy(call, cent_out.at[core], co_s, co_r, device_id=sib, device_id_type=MESH)
    ccopy.start()
    own_out = pltpu.make_async_copy(call, cent_out.at[core], in_sem.at[0])
    own_out.start()
    wait_bytes(sendbuf, asend)
    wait_bytes(sendtag, tsend)
    wait_bytes(rows.at[pl.ds(0, GROUPS)], fsend)
    wait_bytes(tags.at[pl.ds(0, GROUPS)], ftsend)

    def drain(d, carry):
        rows_copy(d).wait()
        p_copy(d).wait()
        p_forward(d).wait()
        return carry

    lax.fori_loop(0, GROUPS, drain, 0)
    ccopy.wait()
    own_out.wait()


def finish(p_ref, rows_ref, cent_ref, cout_ref, rout_ref, chi, clo, res, cent_sem, sem):
    cent_copy = pltpu.make_async_copy(cent_ref, cout_ref, cent_sem)
    cent_copy.start()
    c = cent_ref[...].reshape(chi.shape)
    hi = c.astype(BF16)
    chi[...] = hi
    clo[...] = (c - hi.astype(F32)).astype(BF16)
    copies = []
    for s in range(GROUPS):
        p = p_ref[s].reshape(chi.shape[0], CAP)
        recon = lax.dot_general(p, chi[...], TN, preferred_element_type=F32)
        recon = recon + lax.dot_general(p, clo[...], TN, preferred_element_type=F32)
        res[s] = rows_ref[s].astype(F32) - recon
        copies.append(pltpu.make_async_copy(res.at[s], rout_ref.at[s], sem.at[s]))
        copies[-1].start()
    for copy in copies:
        copy.wait()
    cent_copy.wait()


def per_device(residuals, codes, counts, centroids):
    nrow, width = residuals.shape
    clusters = centroids.shape[1]
    share = clusters // CHIPS
    blocks = 2 * GROUPS
    dma = pltpu.SemaphoreType.DMA
    quarters = CAP // CHUNK
    scratch = [
        pltpu.VMEM((nrow, width), BF16),
        pltpu.VMEM((clusters, width), F32),
        pltpu.VMEM((GROUPS - 1, CAP, width), BF16),
        pltpu.VMEM((GROUPS - 1, 8, CAP), F32),
        pltpu.VMEM((blocks, CAP, width), BF16),
        pltpu.VMEM((blocks, 8, CAP), F32),
        pltpu.VMEM((blocks, clusters, CAP), F32),
        pltpu.VMEM((blocks, 2 * clusters, CAP), BF16),
        pltpu.VMEM((1, clusters), F32),
        pltpu.VMEM((CHIPS - 1, 1, clusters), F32),
        pltpu.VMEM((clusters, width), F32),
        pltpu.VMEM((clusters, width), jnp.int16),
        pltpu.VMEM((CHIPS - 1, share, width), jnp.int16),
        pltpu.VMEM((2, clusters), F32),
        pltpu.VMEM((CHIPS, 2, clusters), F32),
        pltpu.VMEM((clusters, width), F32),
        pltpu.VMEM((clusters, width), jnp.int16),
        pltpu.VMEM((1, clusters), F32),
        pltpu.VMEM((CHIPS - 1, 1, clusters), F32),
        pltpu.VMEM((2 * clusters, width), BF16),
        pltpu.VMEM((clusters, LANES), F32),
        pltpu.VMEM((clusters, LANES), F32),
        pltpu.VMEM((clusters, LANES), F32),
        dma((2,)),
        dma, dma, dma((GROUPS - 1, quarters)), dma((GROUPS - 1,)),
        dma, dma, dma((GROUPS, quarters)), dma((GROUPS,)),
        dma, dma, dma, dma, dma, dma, dma, dma, dma, dma,
        dma((GROUPS,)), dma((GROUPS,)), dma, dma,
        dma((GROUPS,)), dma((GROUPS,)),
    ]
    hbm = pl.BlockSpec(memory_space=pl.ANY)
    vmem = pl.BlockSpec(memory_space=pltpu.VMEM)
    cent, rows, weights = pl.pallas_call(
        kernel,
        out_shape=(
            pltpu.VMEM(centroids.shape, F32),
            pltpu.VMEM((GROUPS, CAP, width), BF16),
            pltpu.VMEM((GROUPS, 2, clusters, CAP), BF16),
        ),
        in_specs=[hbm, vmem, pl.BlockSpec(memory_space=pltpu.SMEM), hbm],
        out_specs=(vmem, vmem, vmem),
        scratch_shapes=scratch,
        compiler_params=pltpu.CompilerParams(
            collective_id=0, has_side_effects=True, vmem_limit_bytes=56 * 1024 * 1024
        ),
    )(residuals, codes.reshape(1, nrow), counts.reshape(GROUPS), centroids)
    both = 2 * clusters
    cent, resid = pl.pallas_call(
        finish,
        out_shape=(
            jax.ShapeDtypeStruct(centroids.shape, F32),
            jax.ShapeDtypeStruct((GROUPS, CAP, width), F32),
        ),
        in_specs=[vmem, vmem, vmem],
        out_specs=(hbm, hbm),
        scratch_shapes=[
            pltpu.VMEM((both, width), BF16),
            pltpu.VMEM((both, width), BF16),
            pltpu.VMEM((GROUPS, CAP, width), F32),
            dma,
            dma((GROUPS,)),
        ],
        compiler_params=pltpu.CompilerParams(vmem_limit_bytes=20 * 1024 * 1024),
    )(weights, rows, cent)
    return cent, resid.reshape(1, 1, GROUPS * CAP, width)


def solution(mesh):
    in_specs = (
        P(("code", "row"), None),
        P(("code", "row")),
        P("code", "row", None),
        P("code", None, None),
    )
    out_specs = (P("code", None, None), P("code", "row", None, None))
    return jax.shard_map(
        per_device, mesh=mesh, in_specs=in_specs, out_specs=out_specs, check_vma=False
    )
```

```python
import jax
import jax.numpy as jnp
from jax import lax
from jax.experimental import pallas as pl
from jax.experimental.pallas import tpu as pltpu
from jax.sharding import PartitionSpec as P

ITERS = 3
SCORE_SCALE = 0.0625
LOG2E = 1.4426950408889634
FULL = 32767.0
MESH = pl.DeviceIdType.MESH
GROUPS = 4
CHIPS = 16
SIDE = 4
FAR_FIRST = sorted(
    [(z, x) for z in range(SIDE) for x in range(SIDE) if z or x],
    key=lambda s: -min(s[0], SIDE - s[0]) - min(s[1], SIDE - s[1]),
)
LANES = 128
CAP = 512
CHUNK = 128
F32 = jnp.float32
BF16 = jnp.bfloat16

NT = (((1,), (1,)), ((), ()))
TN = (((0,), (0,)), ((), ()))


def wait_bytes(ref, sem):
    pltpu.make_async_copy(ref, ref, sem).wait()


def kernel(
    x_hbm, codes_ref, counts_ref, cent_hbm, cent_out, rows_out, p_out,
    x_ref, cent_ref, sendbuf, sendtag, rows, tags, p0, p2, colsend, colrecv, numsend, codesend, numrecv,
    masssend, massrecv, call, callcode, scalesend, scalerecv, c2, cn, colacc, massacc,
    in_sem, asend, tsend, arecv, trecv, fsend, ftsend, frecv, ftrecv,
    col_s, col_r, rs_s, rs_r, m_s, m_r, ag_s, ag_r, sc_s, sc_r, po_s, po_r, co_s, co_r, rows_sem, p_sem,
):
    i = lax.axis_index("code")
    j = lax.axis_index("row")
    core = lax.rem(j, 2)
    chip = lax.div(j, 2)
    cz = lax.div(chip, SIDE)
    cx = lax.rem(chip, SIDE)
    sib = (i, 2 * chip + 1 - core)
    share = numrecv.shape[1]
    clusters = call.shape[0]
    width = call.shape[1]

    peers = [lax.rem(cz + dz, SIDE) * SIDE + lax.rem(cx + dx, SIDE) for dz, dx in FAR_FIRST]

    def chip_at(d):
        return peers[d - 1]

    def row_peer(t):
        return (i, 2 * t + core)

    def group(d):
        return lax.rem(i + d, GROUPS)

    def source(d):
        return lax.rem(i + GROUPS - d, GROUPS)

    load_x = pltpu.make_async_copy(x_hbm, x_ref, in_sem.at[0])
    load_x.start()
    load_c = pltpu.make_async_copy(cent_hbm.at[core], cent_ref, in_sem.at[1])
    load_c.start()

    barrier = pltpu.get_barrier_semaphore()
    for d in range(1, GROUPS):
        pl.semaphore_signal(barrier, inc=1, device_id=(group(d), j), device_id_type=MESH)
    pl.semaphore_signal(barrier, inc=1, device_id=sib, device_id_type=MESH)

    for d in range(1, CHIPS):
        pl.semaphore_signal(barrier, inc=1, device_id=row_peer(chip_at(d)), device_id_type=MESH)

    load_x.wait()
    half = CAP // 2
    iota_r = lax.broadcasted_iota(jnp.int32, (half, x_ref.shape[0]), 1)
    iota_t = lax.broadcasted_iota(jnp.int32, (half, x_ref.shape[0]), 0)
    diff = iota_r - iota_t
    codes8 = jnp.broadcast_to(codes_ref[...], (8, codes_ref.shape[1]))

    def block(d, h):
        target = group(d)
        start = jnp.int32(0)
        for g in range(GROUPS - 1):
            start = start + jnp.where(g < target, counts_ref[g], 0)
        number = counts_ref[target] - h * half
        pick = jnp.where((diff == start + h * half) & (iota_t < number), 1.0, 0.0).astype(BF16)
        piece = jnp.dot(pick, x_ref[...], preferred_element_type=F32).astype(BF16)
        label = (codes8 - 2 * target + 1).astype(F32).astype(BF16)
        tag = lax.dot_general(label, pick, NT, preferred_element_type=F32)
        return piece, tag

    def a2a_copy(d, q):
        lines = pl.ds(q * CHUNK, CHUNK)
        return pltpu.make_async_remote_copy(
            sendbuf.at[d - 1, lines], rows.at[core * GROUPS + d, lines], asend, arecv.at[d - 1, q],
            device_id=(group(d), j), device_id_type=MESH,
        )

    def tag_copy(d):
        return pltpu.make_async_remote_copy(
            sendtag.at[d - 1], tags.at[core * GROUPS + d], tsend, trecv.at[d - 1],
            device_id=(group(d), j), device_id_type=MESH,
        )

    def forward_copy(d, q):
        lines = pl.ds(q * CHUNK, CHUNK)
        return pltpu.make_async_remote_copy(
            rows.at[core * GROUPS + d, lines], rows.at[core * GROUPS + d, lines], fsend, frecv.at[d, q],
            device_id=sib, device_id_type=MESH,
        )

    def forward_tag(d):
        return pltpu.make_async_remote_copy(
            tags.at[core * GROUPS + d], tags.at[core * GROUPS + d], ftsend, ftrecv.at[d],
            device_id=sib, device_id_type=MESH,
        )

    quarters = CAP // CHUNK
    first = True
    for h in range(2):
        for d in (2, 1, 3):
            piece, tag = block(d, h)
            sendbuf[d - 1, h * half : (h + 1) * half, :] = piece
            sendtag[d - 1, :, h * half : (h + 1) * half] = tag
            if first:
                pl.semaphore_wait(barrier, GROUPS - 1 + 1 + CHIPS - 1)
                first = False
            if h == 1:
                tag_copy(d).start()
            for q in range(quarters // 2):
                a2a_copy(d, h * (quarters // 2) + q).start()
    for h in range(2):
        piece, tag = block(0, h)
        rows[core * GROUPS, h * half : (h + 1) * half, :] = piece
        tags[core * GROUPS, :, h * half : (h + 1) * half] = tag
    forward_tag(0).start()

    def own_forward(q, carry):
        forward_copy(0, q).start()
        return carry

    lax.fori_loop(0, quarters, own_forward, 0)

    def split(c):
        hi = c.astype(BF16)
        c2[0:clusters, :] = hi
        c2[clusters : 2 * clusters, :] = (c - hi.astype(F32)).astype(BF16)
        norm = jnp.sum(c * c, axis=1, keepdims=True) * (SCORE_SCALE * LOG2E)
        cn[...] = jnp.broadcast_to(norm, cn.shape)

    def first_soft(parts, n):
        x = [rows[b, pl.ds(lo, n), :] for b, lo in parts]
        x = x[0] if len(x) == 1 else jnp.concatenate(x, axis=0)
        s = lax.dot_general(c2[...], x, NT, preferred_element_type=F32)
        s = s[0:clusters] + s[clusters : 2 * clusters]
        for m, (b, lo) in enumerate(parts):
            for k in range(n // LANES):
                at = pl.ds(lo + k * LANES, LANES)
                first = m * n + k * LANES
                t = s[:, first : first + LANES] * (2.0 * SCORE_SCALE * LOG2E) - cn[...]
                e = jnp.exp2(t - jnp.max(t, axis=0, keepdims=True))
                total = jnp.sum(e, axis=0, keepdims=True)
                live = tags[b, 0:1, at] == (core + 1).astype(F32)
                p = e * jnp.where(live, 1.0 / total, 0.0)
                p0[b, :, at] = p
                colacc[...] += p

    load_c.wait()
    split(cent_ref[...])
    colacc[...] = jnp.zeros_like(colacc)

    other = 1 - core

    first_soft([(core * GROUPS, 0)], CAP)
    forward_tag(0).wait_recv()

    def sib_wait(q, carry):
        forward_copy(0, q).wait_recv()
        return carry

    lax.fori_loop(0, quarters, sib_wait, 0)
    first_soft([(other * GROUPS, 0)], CAP)

    for d in (2, 1, 3):
        tag_copy(d).wait_recv()
        forward_tag(d).start()

    def sib_tag(d, carry):
        forward_tag(d).wait_recv()
        return carry

    lax.fori_loop(1, GROUPS, sib_tag, 0)

    for q in range(quarters):
        for d in (1, 3, 2):
            a2a_copy(d, q).wait_recv()
            forward_copy(d, q).start()
        if q == 0:
            first_soft([(core * GROUPS + d, 0) for d in (1, 3, 2)], CHUNK)
            continue
        for d in (1, 3, 2):
            forward_copy(d, q - 1).wait_recv()
        for d in (1, 3, 2):
            first_soft([(core * GROUPS + d, q * CHUNK), (other * GROUPS + d, (q - 1) * CHUNK)], CHUNK)

    def rows_copy(d):
        return pltpu.make_async_copy(rows.at[core * GROUPS + d], rows_out.at[source(d)], rows_sem.at[d])

    def p_copy(d):
        return pltpu.make_async_copy(
            p2.at[core * GROUPS + d, pl.ds(0, clusters)], p_out.at[source(d), core], p_sem.at[d]
        )

    def p_forward(d):
        return pltpu.make_async_remote_copy(
            p2.at[other * GROUPS + d, pl.ds(0, clusters)], p_out.at[source(d), core], po_s.at[d], po_r.at[d],
            device_id=sib, device_id_type=MESH,
        )

    def rows_start(d, carry):
        rows_copy(d).start()
        return carry

    lax.fori_loop(0, GROUPS, rows_start, 0)
    for d in (1, 3, 2):
        forward_copy(d, quarters - 1).wait_recv()
    first_soft([(other * GROUPS + d, (quarters - 1) * CHUNK) for d in (1, 3, 2)], CHUNK)

    def chunk_of(t):
        return pl.ds(pl.multiple_of(t * share, share), share)

    mine = chunk_of(chip)

    def col_copy(d):
        return pltpu.make_async_remote_copy(
            colsend, colrecv.at[d - 1], col_s, col_r, device_id=row_peer(chip_at(d)), device_id_type=MESH
        )

    def rs_copy(d):
        t = chip_at(d)
        return pltpu.make_async_remote_copy(
            codesend.at[chunk_of(t)], numrecv.at[d - 1], rs_s, rs_r, device_id=row_peer(t), device_id_type=MESH
        )

    def mass_copy(d):
        return pltpu.make_async_remote_copy(
            masssend, massrecv.at[d - 1], m_s, m_r, device_id=row_peer(chip_at(d)), device_id_type=MESH
        )

    def ag_copy(d):
        return pltpu.make_async_remote_copy(
            callcode.at[mine], callcode.at[mine], ag_s, ag_r, device_id=row_peer(chip_at(d)), device_id_type=MESH
        )

    def scale_copy(d):
        return pltpu.make_async_remote_copy(
            scalesend, scalerecv.at[d - 1], sc_s, sc_r, device_id=row_peer(chip_at(d)), device_id_type=MESH
        )

    def encode(v):
        top = jnp.maximum(jnp.max(jnp.abs(v), axis=1, keepdims=True), 1e-34)
        return jnp.round(v * (FULL / top)).astype(jnp.int32).astype(jnp.int16), top * (1.0 / FULL)

    def decode(code, scale):
        return code.astype(jnp.int32).astype(F32) * scale

    def each_peer(make):
        for d in range(1, CHIPS):
            make(d).start()

    blocks = 2 * GROUPS
    rest = pl.ds(0, (CHIPS - 1) * share)

    def as_row(parts):
        return jnp.sum(jnp.transpose(parts), axis=0, keepdims=True)

    def as_column(row):
        return jnp.transpose(jnp.broadcast_to(row, (LANES, clusters)))

    def update(step, carry):
        colsend[...] = as_row(colacc[...])
        each_peer(col_copy)
        massacc[...] = jnp.zeros_like(massacc)
        wait_bytes(colrecv, col_r)
        colacc[...] = as_column(1.0 / (colsend[...] + jnp.sum(colrecv[...], axis=0)))

        def weigh(b, carry):
            for k in range(CAP // LANES):
                at = slice(k * LANES, (k + 1) * LANES)
                q = p0[b, :, at] * colacc[...]
                total = jnp.sum(q, axis=0, keepdims=True)
                live = tags[b, 0:1, at] == (core + 1).astype(F32)
                p = q * jnp.where(live, 1.0 / jnp.where(live, total, 1.0), 0.0)
                hi = p.astype(BF16)
                p2[b, 0:clusters, at] = hi
                p2[b, clusters : 2 * clusters, at] = (p - hi.astype(F32)).astype(BF16)
                massacc[...] += p
            part = jnp.dot(p2[b], rows[b], preferred_element_type=F32)
            numsend[...] += part[0:clusters] + part[clusters : 2 * clusters]
            return carry

        numsend[...] = jnp.zeros_like(numsend)
        lax.fori_loop(0, blocks, weigh, 0, unroll=True)
        code, scale = encode(numsend[...])
        codesend[...] = code
        masssend[0:1, :] = as_row(massacc[...])
        masssend[1:2, :] = jnp.transpose(jnp.broadcast_to(scale, (clusters, LANES)))[0:1, :]
        each_peer(mass_copy)
        each_peer(rs_copy)
        massrecv[CHIPS - 1] = masssend[...]

        @pl.when(step == ITERS - 1)
        def _():
            def p_start(d, carry):
                p_copy(d).start()
                p_forward(d).start()
                return carry

            lax.fori_loop(0, GROUPS, p_start, 0)

        wait_bytes(colrecv, col_s)
        wait_bytes(massrecv.at[pl.ds(0, CHIPS - 1)], m_r)
        massacc[...] = as_column(jnp.sum(massrecv[:, 0:1, :], axis=0))
        scales = jnp.concatenate(
            [massrecv[:, 1, :], jnp.zeros((LANES - CHIPS, clusters), F32)], axis=0
        )
        colacc[...] = jnp.transpose(scales)
        wait_bytes(numrecv, rs_r)
        num = numsend[mine, :]
        for d in range(CHIPS - 1):
            num = num + decode(numrecv[d], colacc[mine, d : d + 1])
        code, scale = encode(num / massacc[mine, 0:1])
        callcode[mine, :] = code
        each_peer(ag_copy)
        massacc[...] = jnp.zeros_like(massacc)
        massacc[mine, :] = jnp.broadcast_to(scale, (share, LANES))
        scalesend[...] = jnp.transpose(massacc[...])[0:1, :]
        each_peer(scale_copy)
        wait_bytes(massrecv.at[pl.ds(0, CHIPS - 1)], m_s)
        wait_bytes(numrecv, rs_s)
        wait_bytes(scalerecv, sc_r)
        colacc[...] = as_column(scalesend[...] + jnp.sum(scalerecv[...], axis=0))
        wait_bytes(callcode.at[rest], ag_r)
        call[...] = decode(callcode[...], colacc[:, 0:1])

        @pl.when(step < ITERS - 1)
        def _():
            split(call[...])
            colacc[...] = jnp.zeros_like(colacc)

            def soft(b, carry):
                first_soft([(b, 0)], CAP)
                return carry

            lax.fori_loop(0, blocks, soft, 0, unroll=True)

        wait_bytes(callcode.at[rest], ag_s)
        wait_bytes(scalerecv, sc_s)
        return carry

    lax.fori_loop(0, ITERS, update, 0)

    ccopy = pltpu.make_async_remote_copy(call, cent_out.at[core], co_s, co_r, device_id=sib, device_id_type=MESH)
    ccopy.start()
    own_out = pltpu.make_async_copy(call, cent_out.at[core], in_sem.at[0])
    own_out.start()
    wait_bytes(sendbuf, asend)
    wait_bytes(sendtag, tsend)
    wait_bytes(rows.at[pl.ds(0, GROUPS)], fsend)
    wait_bytes(tags.at[pl.ds(0, GROUPS)], ftsend)

    def drain(d, carry):
        rows_copy(d).wait()
        p_copy(d).wait()
        p_forward(d).wait()
        return carry

    lax.fori_loop(0, GROUPS, drain, 0)
    ccopy.wait()
    own_out.wait()


def finish(p_ref, rows_ref, cent_ref, cout_ref, rout_ref, chi, clo, res, cent_sem, sem):
    cent_copy = pltpu.make_async_copy(cent_ref, cout_ref, cent_sem)
    cent_copy.start()
    c = cent_ref[...].reshape(chi.shape)
    hi = c.astype(BF16)
    chi[...] = hi
    clo[...] = (c - hi.astype(F32)).astype(BF16)
    copies = []
    for s in range(GROUPS):
        p = p_ref[s].reshape(chi.shape[0], CAP)
        recon = lax.dot_general(p, chi[...], TN, preferred_element_type=F32)
        recon = recon + lax.dot_general(p, clo[...], TN, preferred_element_type=F32)
        res[s] = rows_ref[s].astype(F32) - recon
        copies.append(pltpu.make_async_copy(res.at[s], rout_ref.at[s], sem.at[s]))
        copies[-1].start()
    for copy in copies:
        copy.wait()
    cent_copy.wait()


def per_device(residuals, codes, counts, centroids):
    nrow, width = residuals.shape
    clusters = centroids.shape[1]
    share = clusters // CHIPS
    blocks = 2 * GROUPS
    dma = pltpu.SemaphoreType.DMA
    quarters = CAP // CHUNK
    scratch = [
        pltpu.VMEM((nrow, width), BF16),
        pltpu.VMEM((clusters, width), F32),
        pltpu.VMEM((GROUPS - 1, CAP, width), BF16),
        pltpu.VMEM((GROUPS - 1, 8, CAP), F32),
        pltpu.VMEM((blocks, CAP, width), BF16),
        pltpu.VMEM((blocks, 8, CAP), F32),
        pltpu.VMEM((blocks, clusters, CAP), F32),
        pltpu.VMEM((blocks, 2 * clusters, CAP), BF16),
        pltpu.VMEM((1, clusters), F32),
        pltpu.VMEM((CHIPS - 1, 1, clusters), F32),
        pltpu.VMEM((clusters, width), F32),
        pltpu.VMEM((clusters, width), jnp.int16),
        pltpu.VMEM((CHIPS - 1, share, width), jnp.int16),
        pltpu.VMEM((2, clusters), F32),
        pltpu.VMEM((CHIPS, 2, clusters), F32),
        pltpu.VMEM((clusters, width), F32),
        pltpu.VMEM((clusters, width), jnp.int16),
        pltpu.VMEM((1, clusters), F32),
        pltpu.VMEM((CHIPS - 1, 1, clusters), F32),
        pltpu.VMEM((2 * clusters, width), BF16),
        pltpu.VMEM((clusters, LANES), F32),
        pltpu.VMEM((clusters, LANES), F32),
        pltpu.VMEM((clusters, LANES), F32),
        dma((2,)),
        dma, dma, dma((GROUPS - 1, quarters)), dma((GROUPS - 1,)),
        dma, dma, dma((GROUPS, quarters)), dma((GROUPS,)),
        dma, dma, dma, dma, dma, dma, dma, dma, dma, dma,
        dma((GROUPS,)), dma((GROUPS,)), dma, dma,
        dma((GROUPS,)), dma((GROUPS,)),
    ]
    hbm = pl.BlockSpec(memory_space=pl.ANY)
    vmem = pl.BlockSpec(memory_space=pltpu.VMEM)
    cent, rows, weights = pl.pallas_call(
        kernel,
        out_shape=(
            pltpu.VMEM(centroids.shape, F32),
            pltpu.VMEM((GROUPS, CAP, width), BF16),
            pltpu.VMEM((GROUPS, 2, clusters, CAP), BF16),
        ),
        in_specs=[hbm, vmem, pl.BlockSpec(memory_space=pltpu.SMEM), hbm],
        out_specs=(vmem, vmem, vmem),
        scratch_shapes=scratch,
        compiler_params=pltpu.CompilerParams(
            collective_id=0, has_side_effects=True, vmem_limit_bytes=56 * 1024 * 1024
        ),
    )(residuals, codes.reshape(1, nrow), counts.reshape(GROUPS), centroids)
    both = 2 * clusters
    cent, resid = pl.pallas_call(
        finish,
        out_shape=(
            jax.ShapeDtypeStruct(centroids.shape, F32),
            jax.ShapeDtypeStruct((GROUPS, CAP, width), F32),
        ),
        in_specs=[vmem, vmem, vmem],
        out_specs=(hbm, hbm),
        scratch_shapes=[
            pltpu.VMEM((both, width), BF16),
            pltpu.VMEM((both, width), BF16),
            pltpu.VMEM((GROUPS, CAP, width), F32),
            dma,
            dma((GROUPS,)),
        ],
        compiler_params=pltpu.CompilerParams(vmem_limit_bytes=20 * 1024 * 1024),
    )(weights, rows, cent)
    return cent, resid.reshape(1, 1, GROUPS * CAP, width)


def solution(mesh):
    in_specs = (
        P(("code", "row"), None),
        P(("code", "row")),
        P("code", "row", None),
        P("code", None, None),
    )
    out_specs = (P("code", None, None), P("code", "row", None, None))
    return jax.shard_map(
        per_device, mesh=mesh, in_specs=in_specs, out_specs=out_specs, check_vma=False
    )
```
